256 devices in a mesh: dom: 16 (over z_hi, x, core), edge: 16 (over y, z_lo).
Axes of the slice: x: 4, y: 4, z: 8 (z_hi: 2, z_lo: 4; z = z_hi * 4 + z_lo), core: 2. Of those that a mesh axis runs over, the one named last changes fastest.
Arguments:
- embeddings: float32 [24576, 400], P(('dom', 'edge')), may hold values from -1.5 to 1.5
- adagrad_state: float32 [24576], P(('dom', 'edge')), may hold values from 0.001 to 0.05
- source_rows: int32 [2, 131072], P(None, ('dom', 'edge')), may hold values from 0 to 1535
- target_rows: int32 [2, 131072], P(None, ('dom', 'edge')), may hold values from 0 to 1535
- negative_rows: int32 [2, 256000], P(None, ('dom', 'edge')), may hold values from 0 to 1535
- edge_counts: int32 [2, 256], P(None, ('dom', 'edge')), may hold values from 128 to 512, as said below
Outputs:
- new_embeddings: float32 [24576, 400], P(('dom', 'edge'))
- new_state: float32 [24576], P(('dom', 'edge'))
The draws below stay inside these ranges and needn't reach their ends.
Inputs may be any that keep to these rules, and one draw needn't show every extreme that they name: `edge_counts`: in each round every device has between 128 and 512 live edge slots, its first ones; in each round some device has all 512.
All inputs are finite; a program needn't handle non-finite values.
Results may differ from the reference program's by a relative error of at most 0.0021.
Values may be sent and summed in bfloat16 or wider, within the bound.
A program may use at most 64 MiB of HBM per device.

```python
import math
import jax
import jax.numpy as jnp
import numpy as np
from jax import lax

D = 400
NEG = 1000
ROUNDS = 2
EDGE_DEV = 512
ENT = 1536
ENTITIES = 24576
EDGES = 131072
NEGS = 256000
N_DOM = 16
N_EDGE = 16
DEVICES = 256


def draw_edge_counts(key, part):
    key = jax.random.fold_in(key, 11)
    first_key, second_key = jax.random.split(key)
    counts = jax.random.randint(first_key, (ROUNDS, DEVICES), EDGE_DEV // 4, EDGE_DEV + 1)
    fullest = jax.random.randint(second_key, (ROUNDS, 1), 0, DEVICES)
    columns = jnp.arange(DEVICES, dtype=jnp.int32)[None, :]
    return jnp.where(columns == fullest, EDGE_DEV, counts).astype(jnp.int32)


def with_ends(values, own_key, low, largest):
    shape = values.shape
    index_at = [jax.random.randint(jax.random.fold_in(own_key, axis), (), 0, shape[axis]) for axis in range(len(shape))]
    values = values.at[tuple(index_at)].set(low)
    longest = shape.index(max(shape))
    index_at[longest] = (index_at[longest] + 1) % shape[longest]
    return values.at[tuple(index_at)].set(largest)


def block_levels(key, shape, pieces, smallest, top_value):
    factor_of, own = 1.0, jax.random.fold_in(key, 6)
    for position, blocks in pieces:
        steps = jnp.exp(jax.random.uniform(jax.random.fold_in(own, position), (blocks,), jnp.float32, smallest / len(pieces), top_value / len(pieces)))
        factor_of = factor_of * jnp.repeat(steps, shape[position] // blocks).reshape([-1 if axis == position else 1 for axis in range(len(shape))])
    return factor_of


def gaussian(own_key, dims, spread, bound, cuts=(), held_as=jnp.bfloat16):
    loudness = block_levels(own_key, dims, cuts, -0.22, 0.18) if cuts else 1.0
    drawn = jax.random.normal(own_key, dims, jnp.float32) * spread * loudness
    return jnp.minimum(jnp.maximum(drawn, -bound), bound).astype(held_as)


def setup_inputs(seed: int = 0) -> dict:
    key_list = jax.random.split(jax.random.key(seed), 7)
    embeddings = gaussian(key_list[0], (ENTITIES, D), 0.25, 1.5, ((0, 256),), jnp.float32)
    adagrad_state = jnp.clip(jnp.exp(math.log(0.05) - 3.912023 * jax.random.uniform(key_list[1], (ENTITIES,), jnp.float32) ** block_levels(key_list[1], (ENTITIES,), ((0, 256),), -0.2, 0.2)), 0.001, 0.05)
    source_rows = with_ends(jax.random.randint(key_list[2], (ROUNDS, EDGES), 0, ENT), jax.random.fold_in(key_list[2], 1), 0, ENT - 1).astype(jnp.int32)
    target_rows = with_ends(jax.random.randint(key_list[3], (ROUNDS, EDGES), 0, ENT), jax.random.fold_in(key_list[3], 1), 0, ENT - 1).astype(jnp.int32)
    negative_rows = with_ends(jax.random.randint(key_list[4], (ROUNDS, NEGS), 0, ENT), jax.random.fold_in(key_list[4], 1), 0, ENT - 1).astype(jnp.int32)
    edge_counts = draw_edge_counts(jax.random.fold_in(key_list[6], 71), 0)
    return dict(embeddings=embeddings, adagrad_state=adagrad_state, source_rows=source_rows, target_rows=target_rows, negative_rows=negative_rows, edge_counts=edge_counts)


learning_rate = 0.1

def shard_grads(source_table, target_table, source_idx, target_idx, negative_idx, live_count):
    width = source_table.shape[0]
    columns = jnp.arange(width, dtype=jnp.int32)
    source_hot = (source_idx[:, None] == columns[None, :]).astype(jnp.bfloat16)
    target_hot = (target_idx[:, None] == columns[None, :]).astype(jnp.bfloat16)
    negative_hot = (negative_idx[:, None] == columns[None, :]).astype(jnp.bfloat16)
    sources = jnp.dot(source_hot, source_table, preferred_element_type=jnp.float32).astype(jnp.bfloat16)
    targets = jnp.dot(target_hot, target_table, preferred_element_type=jnp.float32).astype(jnp.bfloat16)
    negatives = jnp.dot(negative_hot, target_table, preferred_element_type=jnp.float32).astype(jnp.bfloat16)
    positive = lax.optimization_barrier(jnp.sum(sources.astype(jnp.float32) * targets.astype(jnp.float32), axis=1))
    negative = jnp.dot(sources, negatives.T, preferred_element_type=jnp.float32)
    live = (jnp.arange(sources.shape[0], dtype=jnp.int32) < live_count).astype(jnp.float32)
    pos_weight = -jax.nn.sigmoid(-positive) * live
    neg_weight = (jax.nn.sigmoid(negative) * live[:, None] / negative.shape[1]).astype(jnp.bfloat16)
    source_grad = (pos_weight[:, None] * targets.astype(jnp.float32) + jnp.dot(neg_weight, negatives, preferred_element_type=jnp.float32)).astype(jnp.bfloat16)
    target_grad = (pos_weight[:, None] * sources.astype(jnp.float32)).astype(jnp.bfloat16)
    negative_grad = jnp.dot(neg_weight.T, sources, preferred_element_type=jnp.float32).astype(jnp.bfloat16)
    table_source = jnp.dot(source_hot.T, source_grad, preferred_element_type=jnp.float32)
    table_target = jnp.dot(target_hot.T, target_grad, preferred_element_type=jnp.float32) + jnp.dot(negative_hot.T, negative_grad, preferred_element_type=jnp.float32)
    return (table_source, table_target)

def reference(embeddings, adagrad_state, source_rows, target_rows, negative_rows, edge_counts):
    table_now = embeddings.reshape(N_DOM, ENT, D)
    accum_now = adagrad_state.reshape(N_DOM, ENT)
    sources_all = source_rows.reshape(ROUNDS, N_DOM, N_EDGE, EDGE_DEV)
    targets_all = target_rows.reshape(ROUNDS, N_DOM, N_EDGE, EDGE_DEV)
    negatives_all = negative_rows.reshape(ROUNDS, N_DOM, N_EDGE, NEG)
    counts_all = edge_counts.reshape(ROUNDS, N_DOM, N_EDGE)
    high_bit = N_DOM.bit_length() - 2
    for round_idx in range(ROUNDS):
        swap_bit = 0 if round_idx % 2 == 0 else high_bit
        partner = np.arange(N_DOM) ^ 1 << swap_bit
        own_tables = table_now.astype(jnp.bfloat16)
        partner_tables = own_tables[partner]

        def add_shard(running, e):
            grads = jax.vmap(shard_grads)(own_tables, partner_tables, sources_all[round_idx, :, e], targets_all[round_idx, :, e], negatives_all[round_idx, :, e], counts_all[round_idx, :, e])
            return ((running[0] + grads[0], running[1] + grads[1]), None)
        empty_grad = jnp.zeros((N_DOM, ENT, D), jnp.float32)
        (grad_source, grad_target), _ = lax.scan(add_shard, (empty_grad, empty_grad), jnp.arange(N_EDGE, dtype=jnp.int32))
        total_grad = grad_source + grad_target[partner]
        accum_now = accum_now + lax.optimization_barrier(jnp.mean(total_grad * total_grad, axis=2))
        table_now = table_now - learning_rate * total_grad / jnp.sqrt(accum_now)[:, :, None]
    return (table_now.reshape(ENTITIES, D), accum_now.reshape(ENTITIES))
```

```python
import jax
import jax.numpy as jnp
from jax import lax
from jax.experimental import pallas as pl
from jax.experimental.pallas import tpu as pltpu
from jax.sharding import PartitionSpec as P

ROUNDS = 2
WIDTH = 400
LANES = 512
MAIN = 384
ROWS = 96
PACKED = 304
SLOTS = 512
BLOCK = 384
ENT = 1536
NEG = 1000
learning_rate = 0.1

MESH = pl.DeviceIdType.MESH
f32 = jnp.float32
bf16 = jnp.bfloat16


def flip(z, k):
    if k == 0:
        return z
    if k == 1:
        return z + 1 - 2 * (z % 2)
    if k == 2:
        return (z + 2) % 4
    return 3 - z


def pack_rest(rest):
    out = rest[0:16, :]
    for g in range(1, 6):
        out = out + pltpu.roll(rest[16 * g : 16 * g + 16, :], 16 * g, 1)
    return out


def rest_piece(rest, g):
    lane = lax.broadcasted_iota(jnp.int32, (16, 128), 1)
    piece = rest if g == 0 else pltpu.roll(rest, 128 - 16 * g, 1)
    return jnp.where(lane < 16, piece, 0.0)


def kernel(
    emb_ref, state_ref, idx_ref, emb_out, state_out,
    E, G, state_col, idx_far, own_pk, Lo, Lp, To, Tp, hot, HS, cnt, MT, tmp,
    PBs, PBr, OBs, OBr, YBs, YBr, GO, ZBs, ZBr, Sv,
    ss, r_own, r_par, r_parq, r_pb, r_ob, r_yb, r_zb, r_idx,
):
    d, e = lax.axis_index("dom"), lax.axis_index("edge")
    zh, x, c = d // 8, (d // 2) % 4, d % 2
    y, z = e // 4, e % 4

    def dev(zh_, c_, y_, z_):
        return (zh_ * 8 + x * 2 + c_, y_ * 4 + z_)

    yp, ym, yo = (y + 1) % 4, (y + 3) % 4, (y + 2) % 4
    up, down, sib = dev(zh, c, yp, z), dev(zh, c, ym, z), dev(zh, 1 - c, y, z)
    mover = zh != c

    barrier = pltpu.get_barrier_semaphore()
    for to in (up, down, sib) + tuple(dev(zh, c, y, flip(z, k)) for k in (1, 2, 3)):
        pl.semaphore_signal(barrier, inc=1, device_id=to, device_id_type=MESH)

    @pl.when(mover)
    def _():
        for k in range(4):
            pl.semaphore_signal(
                barrier, inc=1, device_id=dev(c, zh, y, flip(z, k)), device_id_type=MESH
            )

    started = []
    count = [0]

    def send(src, dst, sem, to, when=None):
        slot = count[0]
        count[0] += 1

        def make():
            return pltpu.make_async_remote_copy(
                src_ref=src, dst_ref=dst, send_sem=ss.at[slot], recv_sem=sem,
                device_id=to, device_id_type=MESH,
            )

        if when is None:
            make().start()
        else:
            pl.when(when)(lambda: make().start())
        started.append((make, when))

    def arrived(dst, sem, when=None):
        def wait():
            pltpu.make_async_remote_copy(
                src_ref=dst, dst_ref=dst, send_sem=ss.at[0], recv_sem=sem,
                device_id=sib, device_id_type=MESH,
            ).wait_recv()

        if when is None:
            wait()
        else:
            pl.when(when)(wait)

    E[:, MAIN:] = jnp.zeros((ROWS, LANES - MAIN), f32)
    E[:, :WIDTH] = emb_ref[...]
    diag = lax.broadcasted_iota(jnp.int32, (ROWS, ROWS), 0) == lax.broadcasted_iota(
        jnp.int32, (ROWS, ROWS), 1
    )
    state_col[...] = jnp.sum(
        jnp.where(diag, jnp.broadcast_to(state_ref[...], (ROWS, ROWS)), 0.0), axis=1, keepdims=True
    )

    def pack_own(r):
        for g in range(3):
            own_pk[r, ROWS * g : ROWS * (g + 1), :] = E[:, 128 * g : 128 * (g + 1)].astype(bf16)
        rest = E[:, MAIN:].astype(bf16).astype(f32)
        own_pk[r, 3 * ROWS :, :] = pack_rest(rest).astype(bf16)

    def row_of(r, i):
        return (idx_ref[0, i : i + 1, :] if r == 0 else idx_far[i : i + 1, :]).astype(f32)

    def source_hot(r):
        column = jnp.transpose(jnp.broadcast_to(row_of(r, 0), (128, SLOTS)))
        lane = lax.broadcasted_iota(jnp.int32, (SLOTS, 128), 1)
        for b, block in enumerate((y, yp, ym, yo)):
            for t in range(3):
                at = (lane + (block * BLOCK + 128 * t)).astype(f32)
                hot[b, :, 128 * t : 128 * (t + 1)] = jnp.where(column == at, 1.0, 0.0).astype(bf16)

    def scatter_hot(r):
        source = row_of(r, 0)
        row = lax.broadcasted_iota(jnp.int32, (128, SLOTS), 0)

        @pl.loop(0, ENT // 128)
        def _(i):
            at = (row + i * 128).astype(f32)
            HS[pl.ds(i * 128, 128), :] = jnp.where(source == at, 1.0, 0.0).astype(bf16)

    def multiplicity(r):
        first, second = row_of(r, 2), row_of(r, 3)
        row = lax.broadcasted_iota(jnp.int32, (128, SLOTS), 0)

        @pl.loop(0, ENT // 128)
        def _(i):
            at = (row + i * 128).astype(f32)
            total = jnp.where(first == at, 1.0, 0.0) + jnp.where(second == at, 1.0, 0.0)
            cnt[pl.ds(i * 128, 128), :] = jnp.sum(total, axis=1, keepdims=True) * (1.0 / NEG)

    def assemble(L, T, r, slot):
        base = slot * ROWS
        for g in range(3):
            T[pl.ds(base, ROWS), 128 * g : 128 * (g + 1)] = L[r, slot, ROWS * g : ROWS * (g + 1), :]
        rest = L[r, slot, 3 * ROWS :, :].astype(f32)
        for g in range(6):
            T[pl.ds(base + 16 * g, 16), MAIN:] = rest_piece(rest, g).astype(bf16)

    def pack_chunk(ref, k):
        base = flip(z, k) * ROWS
        pieces = [ref[pl.ds(base, ROWS), 128 * g : 128 * (g + 1)] for g in range(3)]
        return pieces + [pack_rest(ref[pl.ds(base, ROWS), MAIN:])]

    spans = [(0, ROWS), (ROWS, 2 * ROWS), (2 * ROWS, 3 * ROWS), (3 * ROWS, PACKED)]

    for r in range(ROUNDS):
        far = mover if r == 1 else None
        zt, ct = (zh, c) if r == 0 else (c, zh)
        stay = None if r == 0 else jnp.logical_not(mover)

        pack_own(r)

        def keep(r=r):
            Lo[r, e] = own_pk[r]

        if r == 0:
            keep()
            source_hot(0)
            pl.semaphore_wait(barrier, 6 + 4 * ((zh + c) % 2))
        else:
            pl.when(stay)(keep)
        for k in (3, 2, 1):
            send(own_pk.at[r], Lo.at[r, e], r_own.at[r, e], dev(zt, ct, y, flip(z, k)))
        if r == 1:
            send(own_pk.at[r], Lo.at[r, e], r_own.at[r, e], dev(zt, ct, y, z), mover)

        def line(k):
            slot = y * 4 + flip(z, k)
            if k > 0:
                arrived(Lo.at[r, slot], r_own.at[r, slot])
            elif r == 1:
                arrived(Lo.at[r, slot], r_own.at[r, slot], mover)
            send(Lo.at[r, slot], Lo.at[r, slot], r_own.at[r, slot], up)
            send(Lo.at[r, slot], Lo.at[r, slot], r_own.at[r, slot], down)

        line(0)
        if r == 0:
            send(idx_ref.at[1], idx_far, r_idx.at[0], dev(c, zh, y, z), mover)

            @pl.when(jnp.logical_not(mover))
            def _():
                idx_far[...] = idx_ref[1]

            multiplicity(0)
        for k in (1, 2, 3):
            line(k)
        send(Lo.at[r, pl.ds(y * 4, 4)], Lp.at[r, pl.ds(y * 4, 4)], r_par.at[r, 0], sib)
        if r == 1:
            arrived(idx_far, r_idx.at[0], mover)
            source_hot(1)
        scatter_hot(r)
        for k in range(4):
            slot_m, slot_p = ym * 4 + flip(z, k), yp * 4 + flip(z, k)
            arrived(Lo.at[r, slot_m], r_own.at[r, slot_m])
            if k % 2 == 0:
                send(Lo.at[r, slot_m], Lo.at[r, slot_m], r_own.at[r, slot_m], up)
            arrived(Lo.at[r, slot_p], r_own.at[r, slot_p])
            if k % 2 == 1:
                send(Lo.at[r, slot_p], Lo.at[r, slot_p], r_own.at[r, slot_p], down)
        send(Lo.at[r, pl.ds(ym * 4, 4)], Lp.at[r, pl.ds(ym * 4, 4)], r_par.at[r, 1], sib)
        send(Lo.at[r, pl.ds(yp * 4, 4)], Lp.at[r, pl.ds(yp * 4, 4)], r_par.at[r, 2], sib)
        if r == 1:
            multiplicity(1)

        def sources(b, block, first=False):
            rows = To[pl.ds(pl.multiple_of(block * BLOCK, BLOCK), BLOCK), :]
            part = jnp.dot(hot[b], rows, preferred_element_type=f32)
            Sv[...] = part if first else Sv[...] + part

        for b, block in enumerate((y, yp, ym)):
            for k in range(4):
                assemble(Lo, To, r, block * 4 + k)
            sources(b, block, b == 0)
        for q, block in ((0, y), (1, ym), (2, yp)):
            arrived(Lp.at[r, pl.ds(block * 4, 4)], r_par.at[r, q])
            for k in range(4):
                assemble(Lp, Tp, r, block * 4 + k)
        for k in range(4):
            slot = yo * 4 + flip(z, k)
            arrived(Lo.at[r, slot], r_own.at[r, slot])
            send(Lo.at[r, slot], Lp.at[r, slot], r_parq.at[r, k], sib)
        for k in range(4):
            assemble(Lo, To, r, yo * 4 + k)
        sources(3, yo)
        for k in range(4):
            slot = yo * 4 + flip(z, k)
            arrived(Lp.at[r, slot], r_parq.at[r, k])
            assemble(Lp, Tp, r, slot)

        half = (Sv[...] * 0.5).astype(bf16)
        target = row_of(r, 1)
        slot_at = lax.broadcasted_iota(jnp.int32, (1, SLOTS), 1).astype(f32)
        live = jnp.where(slot_at < row_of(r, 4), 0.5, 0.0)

        def weights(i, held):
            rows = pl.ds(pl.multiple_of(i * BLOCK, BLOCK), BLOCK)
            t = jnp.tanh(
                lax.dot_general(
                    Tp[rows, :], half, (((1,), (1,)), ((), ())), preferred_element_type=f32
                )
            )
            at = (lax.broadcasted_iota(jnp.int32, (BLOCK, SLOTS), 0) + i * BLOCK).astype(f32)
            same = target == at
            m = live * (cnt[rows, :] * (1.0 + t) + jnp.where(same, t - 1.0, 0.0))
            MT[rows, :] = m.astype(bf16)
            return held + jnp.sum(jnp.where(same, m, 0.0), axis=0, keepdims=True)

        held = lax.fori_loop(0, ENT // BLOCK, weights, jnp.zeros((1, SLOTS), f32))
        rounded = held.astype(bf16).astype(f32)
        ratio = jnp.where(rounded == 0.0, 1.0, held / jnp.where(rounded == 0.0, 1.0, rounded))
        ratio = jnp.transpose(jnp.broadcast_to(ratio, (128, SLOTS)))
        ratio = jnp.concatenate([ratio] * (LANES // 128), axis=1)

        scaled = (Sv[...] * ratio).astype(bf16)
        order = (yo, yp, ym, y)
        for b, block in enumerate(order):
            rows = pl.ds(pl.multiple_of(block * BLOCK, BLOCK), BLOCK)
            tmp[...] = jnp.dot(MT[rows, :], scaled, preferred_element_type=f32)
            for k in range(4):
                for (lo, hi), piece in zip(spans, pack_chunk(tmp, k)):
                    PBs[r, b, k, lo:hi, :] = piece.astype(bf16)
            send(PBs.at[r, b], PBr.at[r, b], r_pb.at[r, b], sib)

        grad = lax.dot_general(
            MT[...], Tp[...], (((0,), (0,)), ((), ())), preferred_element_type=f32
        )
        grad = (grad * ratio).astype(bf16)
        for b, block in enumerate(order):
            rows = pl.ds(pl.multiple_of(block * BLOCK, BLOCK), BLOCK)
            tmp[...] = jnp.dot(HS[rows, :], grad, preferred_element_type=f32)
            arrived(PBr.at[r, b], r_pb.at[r, b])
            for k in (3, 2, 1, 0):
                for (lo, hi), piece in zip(spans, pack_chunk(tmp, k)):
                    total = piece + PBr[r, b, k, lo:hi, :].astype(f32)
                    if b == 0:
                        OBs[r, k, lo:hi, :] = total.astype(bf16)
                    elif b < 3 and k % 2 == b % 2:
                        YBs[r, b - 1, k, lo:hi, :] = total.astype(bf16)
                    else:
                        GO[b - 1, k, lo:hi, :] = total
                if b == 0:
                    send(OBs.at[r, k], OBr.at[r, k], r_ob.at[r, k], up if k % 2 == 0 else down)
                elif b < 3 and k % 2 == b % 2:
                    send(
                        YBs.at[r, b - 1, k], YBr.at[r, b - 1, k], r_yb.at[r, b - 1, k],
                        up if b == 1 else down,
                    )
        for k in (3, 2, 1, 0):
            q = k % 2
            arrived(OBr.at[r, k], r_ob.at[r, k])
            YBs[r, q, k] = (GO[q, k] + OBr[r, k].astype(f32)).astype(bf16)
            send(YBs.at[r, q, k], YBr.at[r, q, k], r_yb.at[r, q, k], up if q == 0 else down)
        for k in (3, 2, 1, 0):
            arrived(YBr.at[r, 0, k], r_yb.at[r, 0, k])
            arrived(YBr.at[r, 1, k], r_yb.at[r, 1, k])
            GO[2, k] = GO[2, k] + YBr[r, 0, k].astype(f32) + YBr[r, 1, k].astype(f32)
            if k > 0 or r == 1:
                ZBs[r, k] = GO[2, k].astype(bf16)
                send(
                    ZBs.at[r, k], ZBr.at[r, k], r_zb.at[r, k], dev(zt, ct, y, flip(z, k)),
                    None if k > 0 else mover,
                )
        if r == 1:
            arrived(ZBr.at[r, 0], r_zb.at[r, 0], mover)

            @pl.when(mover)
            def _():
                GO[2, 0] = ZBr[1, 0].astype(f32)

        total = GO[2, 0]
        for k in (1, 2, 3):
            arrived(ZBr.at[r, k], r_zb.at[r, k])
            total = total + ZBr[r, k].astype(f32)

        for g in range(3):
            G[:, 128 * g : 128 * (g + 1)] = total[ROWS * g : ROWS * (g + 1), :]
        for g in range(6):
            G[16 * g : 16 * g + 16, MAIN:] = rest_piece(total[3 * ROWS :, :], g)
        grads = G[...]
        state = state_col[...] + jnp.sum(grads * grads, axis=1, keepdims=True) * (1.0 / WIDTH)
        state_col[...] = state
        E[...] = E[...] - grads * (learning_rate / jnp.sqrt(state))

    emb_out[...] = E[:, :WIDTH]
    state_out[...] = jnp.sum(
        jnp.where(diag, jnp.broadcast_to(state_col[...], (ROWS, ROWS)), 0.0), axis=0, keepdims=True
    )
    for make, when in started:
        if when is None:
            make().wait_send()
        else:
            pl.when(when)(lambda make=make: make().wait_send())


def local(embeddings, adagrad_state, source_rows, target_rows, negative_rows, edge_counts):
    neg = jnp.pad(negative_rows, ((0, 0), (0, 2 * SLOTS - NEG)), constant_values=-1)
    idx = jnp.concatenate(
        [
            source_rows[:, None],
            target_rows[:, None],
            neg.reshape(ROUNDS, 2, SLOTS),
            jnp.broadcast_to(edge_counts[:, :, None], (ROUNDS, 1, SLOTS)),
            jnp.zeros((ROUNDS, 3, SLOTS), jnp.int32),
        ],
        axis=1,
    )
    vmem = pl.BlockSpec(memory_space=pltpu.VMEM)
    DMA = pltpu.SemaphoreType.DMA
    table, state = pl.pallas_call(
        kernel,
        name="bucket_rounds",
        out_shape=(
            jax.ShapeDtypeStruct((ROWS, WIDTH), f32),
            jax.ShapeDtypeStruct((1, ROWS), f32),
        ),
        in_specs=[vmem] * 3,
        out_specs=(vmem, vmem),
        scratch_shapes=[
            pltpu.VMEM((ROWS, LANES), f32),
            pltpu.VMEM((ROWS, LANES), f32),
            pltpu.VMEM((ROWS, 1), f32),
            pltpu.VMEM((8, SLOTS), jnp.int32),
            pltpu.VMEM((ROUNDS, PACKED, 128), bf16),
            pltpu.VMEM((ROUNDS, 16, PACKED, 128), bf16),
            pltpu.VMEM((ROUNDS, 16, PACKED, 128), bf16),
            pltpu.VMEM((ENT, LANES), bf16),
            pltpu.VMEM((ENT, LANES), bf16),
            pltpu.VMEM((4, SLOTS, BLOCK), bf16),
            pltpu.VMEM((ENT, SLOTS), bf16),
            pltpu.VMEM((ENT, 1), f32),
            pltpu.VMEM((ENT, SLOTS), bf16),
            pltpu.VMEM((BLOCK, LANES), f32),
            pltpu.VMEM((ROUNDS, 4, 4, PACKED, 128), bf16),
            pltpu.VMEM((ROUNDS, 4, 4, PACKED, 128), bf16),
            pltpu.VMEM((ROUNDS, 4, PACKED, 128), bf16),
            pltpu.VMEM((ROUNDS, 4, PACKED, 128), bf16),
            pltpu.VMEM((ROUNDS, 2, 4, PACKED, 128), bf16),
            pltpu.VMEM((ROUNDS, 2, 4, PACKED, 128), bf16),
            pltpu.VMEM((3, 4, PACKED, 128), f32),
            pltpu.VMEM((ROUNDS, 4, PACKED, 128), bf16),
            pltpu.VMEM((ROUNDS, 4, PACKED, 128), bf16),
            pltpu.VMEM((SLOTS, LANES), f32),
            DMA((104,)),
            DMA((ROUNDS, 16)),
            DMA((ROUNDS, 3)),
            DMA((ROUNDS, 4)),
            DMA((ROUNDS, 4)),
            DMA((ROUNDS, 4)),
            DMA((ROUNDS, 2, 4)),
            DMA((ROUNDS, 4)),
            DMA((1,)),
        ],
        compiler_params=pltpu.CompilerParams(
            collective_id=0, has_side_effects=True, vmem_limit_bytes=56 * 1024 * 1024
        ),
        cost_estimate=pl.CostEstimate(
            flops=2 * ROUNDS * 5 * ENT * SLOTS * WIDTH,
            bytes_accessed=4 * ROWS * WIDTH * 2,
            transcendentals=ROUNDS * ENT * SLOTS,
        ),
    )(embeddings, adagrad_state.reshape(1, ROWS), idx)
    return table, state.reshape(ROWS)


def solution(mesh):
    in_specs = (
        P(("dom", "edge"), None),
        P(("dom", "edge")),
        P(None, ("dom", "edge")),
        P(None, ("dom", "edge")),
        P(None, ("dom", "edge")),
        P(None, ("dom", "edge")),
    )
    out_specs = (P(("dom", "edge"), None), P(("dom", "edge")))
    return jax.shard_map(local, mesh=mesh, in_specs=in_specs, out_specs=out_specs, check_vma=False)
```

```python
import jax
import jax.numpy as jnp
from jax import lax
from jax.experimental import pallas as pl
from jax.experimental.pallas import tpu as pltpu
from jax.sharding import PartitionSpec as P

ROUNDS = 2
WIDTH = 400
LANES = 512
MAIN = 384
ROWS = 96
PACKED = 304
SLOTS = 512
BLOCK = 384
ENT = 1536
NEG = 1000
learning_rate = 0.1

MESH = pl.DeviceIdType.MESH
f32 = jnp.float32
bf16 = jnp.bfloat16


def flip(z, k):
    if k == 0:
        return z
    if k == 1:
        return z + 1 - 2 * (z % 2)
    if k == 2:
        return (z + 2) % 4
    return 3 - z


def pack_rest(rest):
    out = rest[0:16, :]
    for g in range(1, 6):
        out = out + pltpu.roll(rest[16 * g : 16 * g + 16, :], 16 * g, 1)
    return out


def rest_piece(rest, g):
    lane = lax.broadcasted_iota(jnp.int32, (16, 128), 1)
    piece = rest if g == 0 else pltpu.roll(rest, 128 - 16 * g, 1)
    return jnp.where(lane < 16, piece, 0.0)


def kernel(
    emb_hbm, state_hbm, source_hbm, target_hbm, negative_hbm, count_hbm, emb_out, state_out,
    emb_ref, state_ref, source_ref, target_ref, negative_ref, count_ref, idx_ref, E, G, state_col, idx_far, own_pk, Lo, Lp, To, Tp, hot, HS, cnt, MT, tmp,
    PBs, PBr, OBs, OBr, YBs, YBr, GO, ZBs, ZBr, Sv, Gv,
    ss, r_own, r_par, r_parq, r_pb, r_ob, r_yb, r_zb, r_idx, r_in,
):
    d, e = lax.axis_index("dom"), lax.axis_index("edge")
    zh, x, c = d // 8, (d // 2) % 4, d % 2
    y, z = e // 4, e % 4

    def dev(zh_, c_, y_, z_):
        return (zh_ * 8 + x * 2 + c_, y_ * 4 + z_)

    yp, ym, yo = (y + 1) % 4, (y + 3) % 4, (y + 2) % 4
    up, down, sib = dev(zh, c, yp, z), dev(zh, c, ym, z), dev(zh, 1 - c, y, z)
    mover = zh != c

    barrier = pltpu.get_barrier_semaphore()
    for to in (up, down, sib) + tuple(dev(zh, c, y, flip(z, k)) for k in (1, 2, 3)):
        pl.semaphore_signal(barrier, inc=1, device_id=to, device_id_type=MESH)

    @pl.when(mover)
    def _():
        for k in range(4):
            pl.semaphore_signal(
                barrier, inc=1, device_id=dev(c, zh, y, flip(z, k)), device_id_type=MESH
            )

    started = []
    count = [0]

    def send(src, dst, sem, to, when=None):
        slot = count[0]
        count[0] += 1

        def make():
            return pltpu.make_async_remote_copy(
                src_ref=src, dst_ref=dst, send_sem=ss.at[slot], recv_sem=sem,
                device_id=to, device_id_type=MESH,
            )

        if when is None:
            make().start()
        else:
            pl.when(when)(lambda: make().start())
        started.append((make, when))

    def drain():
        for make, when in started:
            if when is None:
                make().wait_send()
            else:
                pl.when(when)(lambda make=make: make().wait_send())
        started.clear()

    def arrived(dst, sem, when=None):
        def wait():
            pltpu.make_async_remote_copy(
                src_ref=dst, dst_ref=dst, send_sem=ss.at[0], recv_sem=sem,
                device_id=sib, device_id_type=MESH,
            ).wait_recv()

        if when is None:
            wait()
        else:
            pl.when(when)(wait)

    loads = []
    for i, (src, dst) in enumerate(
        (
            (emb_hbm, emb_ref), (state_hbm, state_ref), (source_hbm, source_ref),
            (target_hbm, target_ref), (negative_hbm, negative_ref), (count_hbm, count_ref),
        )
    ):
        loads.append(pltpu.make_async_copy(src, dst, r_in.at[i]))
        loads[-1].start()
    idx_ref[...] = jnp.full((ROUNDS, 8, SLOTS), -1, jnp.int32)
    for load in loads:
        load.wait()
    for r in range(ROUNDS):
        idx_ref[r, 0:1, :] = source_ref[r : r + 1, :]
        idx_ref[r, 1:2, :] = target_ref[r : r + 1, :]
        idx_ref[r, 2:3, :] = negative_ref[r : r + 1, :SLOTS]
        idx_ref[r, 3:4, : NEG - SLOTS] = negative_ref[r : r + 1, SLOTS:]
        idx_ref[r, 4:5, :] = jnp.broadcast_to(count_ref[:, r : r + 1], (1, SLOTS))

    E[:, MAIN:] = jnp.zeros((ROWS, LANES - MAIN), f32)
    E[:, :WIDTH] = emb_ref[...]
    diag = lax.broadcasted_iota(jnp.int32, (ROWS, ROWS), 0) == lax.broadcasted_iota(
        jnp.int32, (ROWS, ROWS), 1
    )
    state_col[...] = jnp.sum(
        jnp.where(diag, jnp.broadcast_to(state_ref[...], (ROWS, ROWS)), 0.0), axis=1, keepdims=True
    )

    def pack_own(r):
        for g in range(3):
            own_pk[r, ROWS * g : ROWS * (g + 1), :] = E[:, 128 * g : 128 * (g + 1)].astype(bf16)
        rest = E[:, MAIN:].astype(bf16).astype(f32)
        own_pk[r, 3 * ROWS :, :] = pack_rest(rest).astype(bf16)

    def row_of(r, i):
        return (idx_ref[0, i : i + 1, :] if r == 0 else idx_far[i : i + 1, :]).astype(f32)

    def source_hot(r):
        column = jnp.transpose(jnp.broadcast_to(row_of(r, 0), (128, SLOTS)))
        lane = lax.broadcasted_iota(jnp.int32, (SLOTS, 128), 1)
        for b, block in enumerate((y, yp, ym, yo)):
            for t in range(3):
                at = (lane + (block * BLOCK + 128 * t)).astype(f32)
                hot[b, :, 128 * t : 128 * (t + 1)] = jnp.where(column == at, 1.0, 0.0).astype(bf16)

    def scatter_hot(r):
        source = row_of(r, 0)
        row = lax.broadcasted_iota(jnp.int32, (128, SLOTS), 0)

        @pl.loop(0, ENT // 128)
        def _(i):
            at = (row + i * 128).astype(f32)
            HS[pl.ds(i * 128, 128), :] = jnp.where(source == at, 1.0, 0.0).astype(bf16)

    def multiplicity(r):
        first, second = row_of(r, 2), row_of(r, 3)
        row = lax.broadcasted_iota(jnp.int32, (128, SLOTS), 0)

        @pl.loop(0, ENT // 128)
        def _(i):
            at = (row + i * 128).astype(f32)
            total = jnp.where(first == at, 1.0, 0.0) + jnp.where(second == at, 1.0, 0.0)
            cnt[pl.ds(i * 128, 128), :] = jnp.sum(total, axis=1, keepdims=True) * (1.0 / NEG)

    def assemble(L, T, r, slot):
        base = slot * ROWS
        for g in range(3):
            T[pl.ds(base, ROWS), 128 * g : 128 * (g + 1)] = L[r, slot, ROWS * g : ROWS * (g + 1), :]
        rest = L[r, slot, 3 * ROWS :, :].astype(f32)
        for g in range(6):
            T[pl.ds(base + 16 * g, 16), MAIN:] = rest_piece(rest, g).astype(bf16)

    def pack_chunk(ref, at):
        base = at * ROWS
        pieces = [ref[pl.ds(base, ROWS), 128 * g : 128 * (g + 1)] for g in range(3)]
        return pieces + [pack_rest(ref[pl.ds(base, ROWS), MAIN:])]

    spans = [(0, ROWS), (ROWS, 2 * ROWS), (2 * ROWS, 3 * ROWS), (3 * ROWS, PACKED)]

    for r in range(ROUNDS):
        far = mover if r == 1 else None
        zt, ct = (zh, c) if r == 0 else (c, zh)
        stay = None if r == 0 else jnp.logical_not(mover)

        pack_own(r)

        def keep(r=r):
            Lo[r, e] = own_pk[r]

        if r == 0:
            keep()
            source_hot(0)
            pl.semaphore_wait(barrier, 6 + 4 * ((zh + c) % 2))
        else:
            pl.when(stay)(keep)
        def place(k, r=r):
            near = flip(z, k)
            return near if r == 0 else near + ((zh + c) % 2) * (3 - 2 * near)

        def turn(k, r=r):
            if k % 2 == 0:
                return flip(z, k)
            a, b = flip(z, k), flip(z, 4 - k)
            return a if r == 0 else a + ((zh + c) % 2) * (b - a)

        for k in range(4):
            if k > 0 or r == 1:
                send(
                    own_pk.at[r], Lo.at[r, e], r_own.at[r, e], dev(zt, ct, y, turn(k)),
                    mover if k == 0 else None,
                )

        def block_wait(block, k, to=None):
            slot = block * 4 + turn(k)
            arrived(Lo.at[r, slot], r_own.at[r, slot])
            if to is not None:
                send(Lo.at[r, slot], Lo.at[r, slot], r_own.at[r, slot], to)

        def line(k):
            slot = y * 4 + turn(k)
            if k > 0:
                arrived(Lo.at[r, slot], r_own.at[r, slot])
            elif r == 1:
                arrived(Lo.at[r, slot], r_own.at[r, slot], mover)
            send(Lo.at[r, slot], Lo.at[r, slot], r_own.at[r, slot], up)
            send(Lo.at[r, slot], Lo.at[r, slot], r_own.at[r, slot], down)

        def sibling_block(block, q):
            send(Lo.at[r, pl.ds(block * 4, 4)], Lp.at[r, pl.ds(block * 4, 4)], r_par.at[r, q], sib)

        def opposite(k):
            slot = yo * 4 + turn(k)
            arrived(Lo.at[r, slot], r_own.at[r, slot])
            send(Lo.at[r, slot], Lp.at[r, slot], r_parq.at[r, turn(k)], sib)

        def sources(b, block):
            for k in range(4):
                assemble(Lo, To, r, block * 4 + k)
            rows = To[pl.ds(pl.multiple_of(block * BLOCK, BLOCK), BLOCK), :]
            part = jnp.dot(hot[b], rows, preferred_element_type=f32)
            Sv[...] = part if b == 0 else Sv[...] + part

        def partner(q, block):
            arrived(Lp.at[r, pl.ds(block * 4, 4)], r_par.at[r, q])
            for k in range(4):
                assemble(Lp, Tp, r, block * 4 + k)

        line(0)
        if r == 0:
            send(idx_ref.at[1], idx_far, r_idx.at[0], dev(c, zh, y, z), mover)

            @pl.when(jnp.logical_not(mover))
            def _():
                idx_far[...] = idx_ref[1]

            multiplicity(0)
        else:
            arrived(idx_far, r_idx.at[0], mover)
            source_hot(1)
        line(1)
        line(2)
        line(3)
        sibling_block(y, 0)
        scatter_hot(r)
        block_wait(ym, 0, up)
        block_wait(yp, 0)
        block_wait(yp, 1, down)
        block_wait(ym, 1)
        block_wait(ym, 2, up)
        block_wait(yp, 2)
        block_wait(yp, 3, down)
        block_wait(ym, 3)
        sibling_block(ym, 1)
        sibling_block(yp, 2)
        opposite(0)
        opposite(1)
        sources(0, y)
        if r == 1:
            multiplicity(1)
        sources(1, yp)
        partner(0, y)
        sources(2, ym)
        partner(1, ym)
        opposite(2)
        opposite(3)
        partner(2, yp)
        sources(3, yo)
        for k in range(4):
            slot = yo * 4 + turn(k)
            arrived(Lp.at[r, slot], r_parq.at[r, turn(k)])
            assemble(Lp, Tp, r, slot)

        half = (Sv[...] * 0.5).astype(bf16)
        target = row_of(r, 1)
        slot_at = lax.broadcasted_iota(jnp.int32, (1, SLOTS), 1).astype(f32)
        live = jnp.where(slot_at < row_of(r, 4), 0.5, 0.0)

        def weights(i, held):
            rows = pl.ds(pl.multiple_of(i * BLOCK, BLOCK), BLOCK)
            t = jnp.tanh(
                lax.dot_general(
                    Tp[rows, :], half, (((1,), (1,)), ((), ())), preferred_element_type=f32
                )
            )
            at = (lax.broadcasted_iota(jnp.int32, (BLOCK, SLOTS), 0) + i * BLOCK).astype(f32)
            same = target == at
            m = live * (cnt[rows, :] * (1.0 + t) + jnp.where(same, t - 1.0, 0.0))
            weight = m.astype(bf16)
            MT[rows, :] = weight
            return held + jnp.sum(jnp.where(same, m, 0.0), axis=0, keepdims=True)

        held = lax.fori_loop(0, ENT // BLOCK, weights, jnp.zeros((1, SLOTS), f32))
        rounded = held.astype(bf16).astype(f32)
        ratio = jnp.where(rounded == 0.0, 1.0, held / jnp.where(rounded == 0.0, 1.0, rounded))
        ratio = jnp.transpose(jnp.broadcast_to(ratio, (128, SLOTS)))
        ratio = jnp.concatenate([ratio] * (LANES // 128), axis=1)

        scaled = (Sv[...] * ratio).astype(bf16)

        def peer(b, block):
            rows = pl.ds(pl.multiple_of(block * BLOCK, BLOCK), BLOCK)
            tmp[...] = jnp.dot(MT[rows, :], scaled, preferred_element_type=f32)
            for k in range(4):
                for (lo, hi), piece in zip(spans, pack_chunk(tmp, k)):
                    PBs[r, b, k, lo:hi, :] = piece.astype(bf16)
            send(PBs.at[r, b], PBr.at[r, b], r_pb.at[r, b], sib)

        def own(b, block):
            rows = pl.ds(pl.multiple_of(block * BLOCK, BLOCK), BLOCK)
            tmp[...] = jnp.dot(HS[rows, :], grad, preferred_element_type=f32)
            arrived(PBr.at[r, b], r_pb.at[r, b])
            for k in (3, 2, 1, 0):
                for (lo, hi), piece in zip(spans, pack_chunk(tmp, place(k))):
                    total = piece + PBr[r, b, place(k), lo:hi, :].astype(f32)
                    if b == 0:
                        OBs[r, k, lo:hi, :] = total.astype(bf16)
                    elif b < 3 and k % 2 == b % 2:
                        YBs[r, b - 1, k, lo:hi, :] = total.astype(bf16)
                    else:
                        GO[b - 1, k, lo:hi, :] = total

        def send_opposite(k):
            send(OBs.at[r, k], OBr.at[r, k], r_ob.at[r, k], up if k % 2 == 0 else down)

        def send_block(q, k):
            send(YBs.at[r, q, k], YBr.at[r, q, k], r_yb.at[r, q, k], up if q == 0 else down)

        def add_opposite(k):
            q = k % 2
            arrived(OBr.at[r, k], r_ob.at[r, k])
            YBs[r, q, k] = (GO[q, k] + OBr[r, k].astype(f32)).astype(bf16)
            send_block(q, k)

        def to_line(k):
            arrived(YBr.at[r, 0, k], r_yb.at[r, 0, k])
            arrived(YBr.at[r, 1, k], r_yb.at[r, 1, k])
            GO[2, k] = GO[2, k] + YBr[r, 0, k].astype(f32) + YBr[r, 1, k].astype(f32)
            if k > 0 or r == 1:
                ZBs[r, k] = GO[2, k].astype(bf16)
                send(
                    ZBs.at[r, k], ZBr.at[r, k], r_zb.at[r, k], dev(zt, ct, y, place(k)),
                    None if k > 0 else mover,
                )

        peer(0, yo)
        grad = lax.dot_general(
            MT[...], Tp[...], (((0,), (0,)), ((), ())), preferred_element_type=f32
        )
        grad = (grad * ratio).astype(bf16)
        own(0, yo)
        send_opposite(3)
        send_opposite(2)
        peer(1, yp)
        peer(2, ym)
        own(1, yp)
        send_block(0, 3)
        own(2, ym)
        send_block(1, 2)
        send_opposite(1)
        send_opposite(0)
        peer(3, y)
        add_opposite(2)
        add_opposite(3)
        send_block(0, 1)
        send_block(1, 0)
        own(3, y)
        to_line(3)
        to_line(2)
        add_opposite(0)
        add_opposite(1)
        to_line(1)
        to_line(0)
        if r == ROUNDS - 1:
            drain()
        if r == 1:
            arrived(ZBr.at[r, 0], r_zb.at[r, 0], mover)

            @pl.when(mover)
            def _():
                GO[2, 0] = ZBr[1, 0].astype(f32)

        total = GO[2, 0]
        for k in (1, 2, 3):
            arrived(ZBr.at[r, k], r_zb.at[r, k])
            total = total + ZBr[r, k].astype(f32)

        for g in range(3):
            G[:, 128 * g : 128 * (g + 1)] = total[ROWS * g : ROWS * (g + 1), :]
        for g in range(6):
            G[16 * g : 16 * g + 16, MAIN:] = rest_piece(total[3 * ROWS :, :], g)
        grads = G[...]
        state = state_col[...] + jnp.sum(grads * grads, axis=1, keepdims=True) * (1.0 / WIDTH)
        state_col[...] = state
        E[...] = E[...] - grads * (learning_rate / jnp.sqrt(state))

    emb_out[...] = E[:, :WIDTH]
    state_out[...] = jnp.sum(
        jnp.where(diag, jnp.broadcast_to(state_col[...], (ROWS, ROWS)), 0.0), axis=0, keepdims=True
    )
    drain()


def local(embeddings, adagrad_state, source_rows, target_rows, negative_rows, edge_counts):
    vmem = pl.BlockSpec(memory_space=pltpu.VMEM)
    DMA = pltpu.SemaphoreType.DMA
    table, state = pl.pallas_call(
        kernel,
        name="bucket_rounds",
        out_shape=(
            pltpu.VMEM((ROWS, WIDTH), f32),
            pltpu.VMEM((1, ROWS), f32),
        ),
        in_specs=[pl.BlockSpec(memory_space=pl.ANY)] * 6,
        out_specs=(vmem, vmem),
        scratch_shapes=[
            pltpu.VMEM((ROWS, WIDTH), f32),
            pltpu.VMEM((1, ROWS), f32),
            pltpu.VMEM((ROUNDS, SLOTS), jnp.int32),
            pltpu.VMEM((ROUNDS, SLOTS), jnp.int32),
            pltpu.VMEM((ROUNDS, NEG), jnp.int32),
            pltpu.VMEM((1, ROUNDS), jnp.int32),
            pltpu.VMEM((ROUNDS, 8, SLOTS), jnp.int32),
            pltpu.VMEM((ROWS, LANES), f32),
            pltpu.VMEM((ROWS, LANES), f32),
            pltpu.VMEM((ROWS, 1), f32),
            pltpu.VMEM((8, SLOTS), jnp.int32),
            pltpu.VMEM((ROUNDS, PACKED, 128), bf16),
            pltpu.VMEM((ROUNDS, 16, PACKED, 128), bf16),
            pltpu.VMEM((ROUNDS, 16, PACKED, 128), bf16),
            pltpu.VMEM((ENT, LANES), bf16),
            pltpu.VMEM((ENT, LANES), bf16),
            pltpu.VMEM((4, SLOTS, BLOCK), bf16),
            pltpu.VMEM((ENT, SLOTS), bf16),
            pltpu.VMEM((ENT, 1), f32),
            pltpu.VMEM((ENT, SLOTS), bf16),
            pltpu.VMEM((BLOCK, LANES), f32),
            pltpu.VMEM((ROUNDS, 4, 4, PACKED, 128), bf16),
            pltpu.VMEM((ROUNDS, 4, 4, PACKED, 128), bf16),
            pltpu.VMEM((ROUNDS, 4, PACKED, 128), bf16),
            pltpu.VMEM((ROUNDS, 4, PACKED, 128), bf16),
            pltpu.VMEM((ROUNDS, 2, 4, PACKED, 128), bf16),
            pltpu.VMEM((ROUNDS, 2, 4, PACKED, 128), bf16),
            pltpu.VMEM((3, 4, PACKED, 128), f32),
            pltpu.VMEM((ROUNDS, 4, PACKED, 128), bf16),
            pltpu.VMEM((ROUNDS, 4, PACKED, 128), bf16),
            pltpu.VMEM((SLOTS, LANES), f32),
            pltpu.VMEM((SLOTS, LANES), f32),
            DMA((104,)),
            DMA((ROUNDS, 16)),
            DMA((ROUNDS, 3)),
            DMA((ROUNDS, 4)),
            DMA((ROUNDS, 4)),
            DMA((ROUNDS, 4)),
            DMA((ROUNDS, 2, 4)),
            DMA((ROUNDS, 4)),
            DMA((1,)),
            DMA((6,)),
        ],
        compiler_params=pltpu.CompilerParams(
            collective_id=0, has_side_effects=True, vmem_limit_bytes=56 * 1024 * 1024
        ),
        cost_estimate=pl.CostEstimate(
            flops=2 * ROUNDS * 5 * ENT * SLOTS * WIDTH,
            bytes_accessed=4 * ROWS * WIDTH * 2,
            transcendentals=ROUNDS * ENT * SLOTS,
        ),
    )(
        embeddings,
        adagrad_state.reshape(1, ROWS),
        source_rows,
        target_rows,
        negative_rows,
        edge_counts.reshape(1, ROUNDS),
    )
    return table, state.reshape(ROWS)


def solution(mesh):
    in_specs = (
        P(("dom", "edge"), None),
        P(("dom", "edge")),
        P(None, ("dom", "edge")),
        P(None, ("dom", "edge")),
        P(None, ("dom", "edge")),
        P(None, ("dom", "edge")),
    )
    out_specs = (P(("dom", "edge"), None), P(("dom", "edge")))
    return jax.shard_map(local, mesh=mesh, in_specs=in_specs, out_specs=out_specs, check_vma=False)
```

```python
import jax
import jax.numpy as jnp
from jax import lax
from jax.experimental import pallas as pl
from jax.experimental.pallas import tpu as pltpu
from jax.sharding import PartitionSpec as P

ROUNDS = 2
WIDTH = 400
LANES = 512
MAIN = 384
ROWS = 96
PACKED = 304
SLOTS = 512
BLOCK = 384
ENT = 1536
NEG = 1000
learning_rate = 0.1

MESH = pl.DeviceIdType.MESH
f32 = jnp.float32
bf16 = jnp.bfloat16


def flip(z, k):
    if k == 0:
        return z
    if k == 1:
        return z + 1 - 2 * (z % 2)
    if k == 2:
        return (z + 2) % 4
    return 3 - z


def pack_rest(rest):
    out = rest[0:16, :]
    for g in range(1, 6):
        out = out + pltpu.roll(rest[16 * g : 16 * g + 16, :], 16 * g, 1)
    return out


def rest_piece(rest, g):
    lane = lax.broadcasted_iota(jnp.int32, (16, 128), 1)
    piece = rest if g == 0 else pltpu.roll(rest, 128 - 16 * g, 1)
    return jnp.where(lane < 16, piece, 0.0)


def kernel(
    emb_hbm, state_hbm, source_hbm, target_hbm, negative_hbm, count_hbm, emb_out, state_out,
    emb_ref, state_ref, source_ref, target_ref, negative_ref, count_ref, idx_ref, E, G, state_col, idx_far, own_pk, Lo, Lp, To, Tp, hot, HS, Us, Ws, MT, tmp,
    PBs, PBr, OBs, OBr, YBs, YBr, GO, ZBs, ZBr, Sv, Gv,
    ss, r_own, r_par, r_parq, r_pb, r_ob, r_yb, r_zb, r_idx, r_in,
):
    d, e = lax.axis_index("dom"), lax.axis_index("edge")
    zh, x, c = d // 8, (d // 2) % 4, d % 2
    y, z = e // 4, e % 4

    def dev(zh_, c_, y_, z_):
        return (zh_ * 8 + x * 2 + c_, y_ * 4 + z_)

    yp, ym, yo = (y + 1) % 4, (y + 3) % 4, (y + 2) % 4
    up, down, sib = dev(zh, c, yp, z), dev(zh, c, ym, z), dev(zh, 1 - c, y, z)
    mover = zh != c

    barrier = pltpu.get_barrier_semaphore()
    for to in (up, down, sib) + tuple(dev(zh, c, y, flip(z, k)) for k in (1, 2, 3)):
        pl.semaphore_signal(barrier, inc=1, device_id=to, device_id_type=MESH)

    @pl.when(mover)
    def _():
        for k in range(4):
            pl.semaphore_signal(
                barrier, inc=1, device_id=dev(c, zh, y, flip(z, k)), device_id_type=MESH
            )

    started = []
    count = [0]

    def send(src, dst, sem, to, when=None):
        slot = count[0]
        count[0] += 1

        def make():
            return pltpu.make_async_remote_copy(
                src_ref=src, dst_ref=dst, send_sem=ss.at[slot], recv_sem=sem,
                device_id=to, device_id_type=MESH,
            )

        if when is None:
            make().start()
        else:
            pl.when(when)(lambda: make().start())
        started.append((make, when))

    def drain():
        for make, when in started:
            if when is None:
                make().wait_send()
            else:
                pl.when(when)(lambda make=make: make().wait_send())
        started.clear()

    def arrived(dst, sem, when=None):
        def wait():
            pltpu.make_async_remote_copy(
                src_ref=dst, dst_ref=dst, send_sem=ss.at[0], recv_sem=sem,
                device_id=sib, device_id_type=MESH,
            ).wait_recv()

        if when is None:
            wait()
        else:
            pl.when(when)(wait)

    loads = []
    for i, (src, dst) in enumerate(
        (
            (emb_hbm, emb_ref), (state_hbm, state_ref), (source_hbm, source_ref),
            (target_hbm, target_ref), (negative_hbm, negative_ref), (count_hbm, count_ref),
        )
    ):
        loads.append(pltpu.make_async_copy(src, dst, r_in.at[i]))
        loads[-1].start()
    idx_ref[...] = jnp.full((ROUNDS, 8, SLOTS), -1, jnp.int32)
    for load in loads:
        load.wait()
    for r in range(ROUNDS):
        idx_ref[r, 0:1, :] = source_ref[r : r + 1, :]
        idx_ref[r, 1:2, :] = target_ref[r : r + 1, :]
        idx_ref[r, 2:3, :] = negative_ref[r : r + 1, :SLOTS]
        idx_ref[r, 3:4, : NEG - SLOTS] = negative_ref[r : r + 1, SLOTS:]
        idx_ref[r, 4:5, :] = jnp.broadcast_to(count_ref[:, r : r + 1], (1, SLOTS))

    E[:, MAIN:] = jnp.zeros((ROWS, LANES - MAIN), f32)
    E[:, :WIDTH] = emb_ref[...]
    diag = lax.broadcasted_iota(jnp.int32, (ROWS, ROWS), 0) == lax.broadcasted_iota(
        jnp.int32, (ROWS, ROWS), 1
    )
    state_col[...] = jnp.sum(
        jnp.where(diag, jnp.broadcast_to(state_ref[...], (ROWS, ROWS)), 0.0), axis=1, keepdims=True
    )

    def pack_own(r):
        for g in range(3):
            own_pk[r, ROWS * g : ROWS * (g + 1), :] = E[:, 128 * g : 128 * (g + 1)].astype(bf16)
        rest = E[:, MAIN:].astype(bf16).astype(f32)
        own_pk[r, 3 * ROWS :, :] = pack_rest(rest).astype(bf16)

    def row_of(r, i):
        return (idx_ref[0, i : i + 1, :] if r == 0 else idx_far[i : i + 1, :]).astype(f32)

    def source_hot(r):
        column = jnp.transpose(jnp.broadcast_to(row_of(r, 0), (128, SLOTS)))
        lane = lax.broadcasted_iota(jnp.int32, (SLOTS, 128), 1)
        for b, block in enumerate((y, yp, ym, yo)):
            for t in range(3):
                at = (lane + (block * BLOCK + 128 * t)).astype(f32)
                hot[b, :, 128 * t : 128 * (t + 1)] = jnp.where(column == at, 1.0, 0.0).astype(bf16)

    def scatter_hot(r):
        source = row_of(r, 0)
        row = lax.broadcasted_iota(jnp.int32, (128, SLOTS), 0)

        @pl.loop(0, ENT // 128)
        def _(i):
            at = (row + i * 128).astype(f32)
            HS[pl.ds(i * 128, 128), :] = jnp.where(source == at, 1.0, 0.0).astype(bf16)

    def multiplicity(r):
        first, second = row_of(r, 2), row_of(r, 3)
        target = row_of(r, 1)
        slot_at = lax.broadcasted_iota(jnp.int32, (1, SLOTS), 1).astype(f32)
        live = jnp.where(slot_at < row_of(r, 4), 0.5, 0.0)
        row = lax.broadcasted_iota(jnp.int32, (128, SLOTS), 0)

        @pl.loop(0, ENT // 128)
        def _(i):
            at = (row + i * 128).astype(f32)
            total = jnp.where(first == at, 1.0, 0.0) + jnp.where(second == at, 1.0, 0.0)
            share = jnp.sum(total, axis=1, keepdims=True) * (1.0 / NEG)
            same = jnp.where(target == at, 1.0, 0.0)
            Us[pl.ds(i * 128, 128), :] = live * (share + same)
            Ws[pl.ds(i * 128, 128), :] = live * (share - same)

    def assemble(L, T, r, slot):
        base = slot * ROWS
        for g in range(3):
            T[pl.ds(base, ROWS), 128 * g : 128 * (g + 1)] = L[r, slot, ROWS * g : ROWS * (g + 1), :]
        rest = L[r, slot, 3 * ROWS :, :].astype(f32)
        for g in range(6):
            T[pl.ds(base + 16 * g, 16), MAIN:] = rest_piece(rest, g).astype(bf16)

    def pack_chunk(ref, at):
        base = at * ROWS
        pieces = [ref[pl.ds(base, ROWS), 128 * g : 128 * (g + 1)] for g in range(3)]
        return pieces + [pack_rest(ref[pl.ds(base, ROWS), MAIN:])]

    spans = [(0, ROWS), (ROWS, 2 * ROWS), (2 * ROWS, 3 * ROWS), (3 * ROWS, PACKED)]

    for r in range(ROUNDS):
        far = mover if r == 1 else None
        zt, ct = (zh, c) if r == 0 else (c, zh)
        stay = None if r == 0 else jnp.logical_not(mover)

        pack_own(r)

        def keep(r=r):
            Lo[r, e] = own_pk[r]

        if r == 0:
            keep()
            source_hot(0)
            pl.semaphore_wait(barrier, 6 + 4 * ((zh + c) % 2))
        else:
            pl.when(stay)(keep)
        def place(k, r=r):
            near = flip(z, k)
            return near if r == 0 else near + ((zh + c) % 2) * (3 - 2 * near)

        def turn(k, r=r):
            if k % 2 == 0:
                return flip(z, k)
            a, b = flip(z, k), flip(z, 4 - k)
            return a if r == 0 else a + ((zh + c) % 2) * (b - a)

        for k in range(4):
            if k > 0 or r == 1:
                send(
                    own_pk.at[r], Lo.at[r, e], r_own.at[r, e], dev(zt, ct, y, turn(k)),
                    mover if k == 0 else None,
                )

        def block_wait(block, k, to=None):
            slot = block * 4 + turn(k)
            arrived(Lo.at[r, slot], r_own.at[r, slot])
            if to is not None:
                send(Lo.at[r, slot], Lo.at[r, slot], r_own.at[r, slot], to)

        def line(k):
            slot = y * 4 + turn(k)
            if k > 0:
                arrived(Lo.at[r, slot], r_own.at[r, slot])
            elif r == 1:
                arrived(Lo.at[r, slot], r_own.at[r, slot], mover)
            send(Lo.at[r, slot], Lo.at[r, slot], r_own.at[r, slot], up)
            send(Lo.at[r, slot], Lo.at[r, slot], r_own.at[r, slot], down)

        def sibling_block(block, q):
            send(Lo.at[r, pl.ds(block * 4, 4)], Lp.at[r, pl.ds(block * 4, 4)], r_par.at[r, q], sib)

        def opposite(k):
            slot = yo * 4 + turn(k)
            arrived(Lo.at[r, slot], r_own.at[r, slot])
            send(Lo.at[r, slot], Lp.at[r, slot], r_parq.at[r, turn(k)], sib)

        def sources(b, block):
            for k in range(4):
                assemble(Lo, To, r, block * 4 + k)
            rows = To[pl.ds(pl.multiple_of(block * BLOCK, BLOCK), BLOCK), :]
            part = jnp.dot(hot[b], rows, preferred_element_type=f32)
            Sv[...] = part if b == 0 else Sv[...] + part

        def partner(q, block):
            arrived(Lp.at[r, pl.ds(block * 4, 4)], r_par.at[r, q])
            for k in range(4):
                assemble(Lp, Tp, r, block * 4 + k)

        line(0)
        if r == 0:
            send(idx_ref.at[1], idx_far, r_idx.at[0], dev(c, zh, y, z), mover)

            @pl.when(jnp.logical_not(mover))
            def _():
                idx_far[...] = idx_ref[1]

            multiplicity(0)
        else:
            arrived(idx_far, r_idx.at[0], mover)
            source_hot(1)
        line(1)
        line(2)
        line(3)
        sibling_block(y, 0)
        scatter_hot(r)
        block_wait(ym, 0, up)
        block_wait(yp, 0)
        block_wait(yp, 1, down)
        block_wait(ym, 1)
        block_wait(ym, 2, up)
        block_wait(yp, 2)
        block_wait(yp, 3, down)
        block_wait(ym, 3)
        sibling_block(ym, 1)
        sibling_block(yp, 2)
        opposite(0)
        opposite(1)
        sources(0, y)
        if r == 1:
            multiplicity(1)
        sources(1, yp)
        partner(0, y)
        sources(2, ym)
        partner(1, ym)
        opposite(2)
        opposite(3)
        partner(2, yp)
        sources(3, yo)
        for k in range(4):
            slot = yo * 4 + turn(k)
            arrived(Lp.at[r, slot], r_parq.at[r, turn(k)])
            assemble(Lp, Tp, r, slot)

        half = (Sv[...] * 0.5).astype(bf16)
        def weights(i, held):
            rows = pl.ds(pl.multiple_of(i * BLOCK, BLOCK), BLOCK)
            t = jnp.tanh(
                lax.dot_general(
                    Tp[rows, :], half, (((1,), (1,)), ((), ())), preferred_element_type=f32
                )
            )
            slope, level = Us[rows, :], Ws[rows, :]
            m = slope * t + level
            weight = m.astype(bf16)
            MT[rows, :] = weight
            return held + jnp.sum((slope - level) * m, axis=0, keepdims=True)

        held = lax.fori_loop(0, ENT // BLOCK, weights, jnp.zeros((1, SLOTS), f32), unroll=True)
        rounded = held.astype(bf16).astype(f32)
        ratio = jnp.where(rounded == 0.0, 1.0, held / jnp.where(rounded == 0.0, 1.0, rounded))
        ratio = jnp.transpose(jnp.broadcast_to(ratio, (128, SLOTS)))
        ratio = jnp.concatenate([ratio] * (LANES // 128), axis=1)

        scaled = (Sv[...] * ratio).astype(bf16)

        def peer(b, block):
            rows = pl.ds(pl.multiple_of(block * BLOCK, BLOCK), BLOCK)
            tmp[...] = jnp.dot(MT[rows, :], scaled, preferred_element_type=f32)
            for k in range(4):
                for (lo, hi), piece in zip(spans, pack_chunk(tmp, k)):
                    PBs[r, b, k, lo:hi, :] = piece.astype(bf16)
            send(PBs.at[r, b], PBr.at[r, b], r_pb.at[r, b], sib)

        def own(b, block):
            rows = pl.ds(pl.multiple_of(block * BLOCK, BLOCK), BLOCK)
            tmp[...] = jnp.dot(HS[rows, :], grad, preferred_element_type=f32)
            arrived(PBr.at[r, b], r_pb.at[r, b])
            for k in (3, 2, 1, 0):
                for (lo, hi), piece in zip(spans, pack_chunk(tmp, place(k))):
                    total = piece + PBr[r, b, place(k), lo:hi, :].astype(f32)
                    if b == 0:
                        OBs[r, k, lo:hi, :] = total.astype(bf16)
                    elif b < 3 and k % 2 == b % 2:
                        YBs[r, b - 1, k, lo:hi, :] = total.astype(bf16)
                    else:
                        GO[b - 1, k, lo:hi, :] = total

        def send_opposite(k):
            send(OBs.at[r, k], OBr.at[r, k], r_ob.at[r, k], up if k % 2 == 0 else down)

        def send_block(q, k):
            send(YBs.at[r, q, k], YBr.at[r, q, k], r_yb.at[r, q, k], up if q == 0 else down)

        def add_opposite(k):
            q = k % 2
            arrived(OBr.at[r, k], r_ob.at[r, k])
            YBs[r, q, k] = (GO[q, k] + OBr[r, k].astype(f32)).astype(bf16)
            send_block(q, k)

        def to_line(k):
            arrived(YBr.at[r, 0, k], r_yb.at[r, 0, k])
            arrived(YBr.at[r, 1, k], r_yb.at[r, 1, k])
            GO[2, k] = GO[2, k] + YBr[r, 0, k].astype(f32) + YBr[r, 1, k].astype(f32)
            if k > 0 or r == 1:
                ZBs[r, k] = GO[2, k].astype(bf16)
                send(
                    ZBs.at[r, k], ZBr.at[r, k], r_zb.at[r, k], dev(zt, ct, y, place(k)),
                    None if k > 0 else mover,
                )

        peer(0, yo)
        grad = lax.dot_general(
            MT[...], Tp[...], (((0,), (0,)), ((), ())), preferred_element_type=f32
        )
        grad = (grad * ratio).astype(bf16)
        own(0, yo)
        send_opposite(3)
        send_opposite(2)
        peer(1, yp)
        peer(2, ym)
        own(1, yp)
        send_block(0, 3)
        own(2, ym)
        send_block(1, 2)
        send_opposite(1)
        send_opposite(0)
        peer(3, y)
        add_opposite(2)
        add_opposite(3)
        send_block(0, 1)
        send_block(1, 0)
        own(3, y)
        to_line(3)
        to_line(2)
        add_opposite(0)
        add_opposite(1)
        to_line(1)
        to_line(0)
        if r == ROUNDS - 1:
            drain()
        if r == 1:
            arrived(ZBr.at[r, 0], r_zb.at[r, 0], mover)

            @pl.when(mover)
            def _():
                GO[2, 0] = ZBr[1, 0].astype(f32)

        total = GO[2, 0]
        for k in (1, 2, 3):
            arrived(ZBr.at[r, k], r_zb.at[r, k])
            total = total + ZBr[r, k].astype(f32)

        for g in range(3):
            G[:, 128 * g : 128 * (g + 1)] = total[ROWS * g : ROWS * (g + 1), :]
        for g in range(6):
            G[16 * g : 16 * g + 16, MAIN:] = rest_piece(total[3 * ROWS :, :], g)
        grads = G[...]
        state = state_col[...] + jnp.sum(grads * grads, axis=1, keepdims=True) * (1.0 / WIDTH)
        state_col[...] = state
        E[...] = E[...] - grads * (learning_rate / jnp.sqrt(state))

    emb_out[...] = E[:, :WIDTH]
    state_out[...] = jnp.sum(
        jnp.where(diag, jnp.broadcast_to(state_col[...], (ROWS, ROWS)), 0.0), axis=0, keepdims=True
    )
    drain()


def local(embeddings, adagrad_state, source_rows, target_rows, negative_rows, edge_counts):
    vmem = pl.BlockSpec(memory_space=pltpu.VMEM)
    DMA = pltpu.SemaphoreType.DMA
    table, state = pl.pallas_call(
        kernel,
        name="bucket_rounds",
        out_shape=(
            pltpu.VMEM((ROWS, WIDTH), f32),
            pltpu.VMEM((1, ROWS), f32),
        ),
        in_specs=[pl.BlockSpec(memory_space=pl.ANY)] * 6,
        out_specs=(vmem, vmem),
        scratch_shapes=[
            pltpu.VMEM((ROWS, WIDTH), f32),
            pltpu.VMEM((1, ROWS), f32),
            pltpu.VMEM((ROUNDS, SLOTS), jnp.int32),
            pltpu.VMEM((ROUNDS, SLOTS), jnp.int32),
            pltpu.VMEM((ROUNDS, NEG), jnp.int32),
            pltpu.VMEM((1, ROUNDS), jnp.int32),
            pltpu.VMEM((ROUNDS, 8, SLOTS), jnp.int32),
            pltpu.VMEM((ROWS, LANES), f32),
            pltpu.VMEM((ROWS, LANES), f32),
            pltpu.VMEM((ROWS, 1), f32),
            pltpu.VMEM((8, SLOTS), jnp.int32),
            pltpu.VMEM((ROUNDS, PACKED, 128), bf16),
            pltpu.VMEM((ROUNDS, 16, PACKED, 128), bf16),
            pltpu.VMEM((ROUNDS, 16, PACKED, 128), bf16),
            pltpu.VMEM((ENT, LANES), bf16),
            pltpu.VMEM((ENT, LANES), bf16),
            pltpu.VMEM((4, SLOTS, BLOCK), bf16),
            pltpu.VMEM((ENT, SLOTS), bf16),
            pltpu.VMEM((ENT, SLOTS), f32),
            pltpu.VMEM((ENT, SLOTS), f32),
            pltpu.VMEM((ENT, SLOTS), bf16),
            pltpu.VMEM((BLOCK, LANES), f32),
            pltpu.VMEM((ROUNDS, 4, 4, PACKED, 128), bf16),
            pltpu.VMEM((ROUNDS, 4, 4, PACKED, 128), bf16),
            pltpu.VMEM((ROUNDS, 4, PACKED, 128), bf16),
            pltpu.VMEM((ROUNDS, 4, PACKED, 128), bf16),
            pltpu.VMEM((ROUNDS, 2, 4, PACKED, 128), bf16),
            pltpu.VMEM((ROUNDS, 2, 4, PACKED, 128), bf16),
            pltpu.VMEM((3, 4, PACKED, 128), f32),
            pltpu.VMEM((ROUNDS, 4, PACKED, 128), bf16),
            pltpu.VMEM((ROUNDS, 4, PACKED, 128), bf16),
            pltpu.VMEM((SLOTS, LANES), f32),
            pltpu.VMEM((SLOTS, LANES), f32),
            DMA((104,)),
            DMA((ROUNDS, 16)),
            DMA((ROUNDS, 3)),
            DMA((ROUNDS, 4)),
            DMA((ROUNDS, 4)),
            DMA((ROUNDS, 4)),
            DMA((ROUNDS, 2, 4)),
            DMA((ROUNDS, 4)),
            DMA((1,)),
            DMA((6,)),
        ],
        compiler_params=pltpu.CompilerParams(
            collective_id=0, has_side_effects=True, vmem_limit_bytes=56 * 1024 * 1024
        ),
        cost_estimate=pl.CostEstimate(
            flops=2 * ROUNDS * 5 * ENT * SLOTS * WIDTH,
            bytes_accessed=4 * ROWS * WIDTH * 2,
            transcendentals=ROUNDS * ENT * SLOTS,
        ),
    )(
        embeddings,
        adagrad_state.reshape(1, ROWS),
        source_rows,
        target_rows,
        negative_rows,
        edge_counts.reshape(1, ROUNDS),
    )
    return table, state.reshape(ROWS)


def solution(mesh):
    in_specs = (
        P(("dom", "edge"), None),
        P(("dom", "edge")),
        P(None, ("dom", "edge")),
        P(None, ("dom", "edge")),
        P(None, ("dom", "edge")),
        P(None, ("dom", "edge")),
    )
    out_specs = (P(("dom", "edge"), None), P(("dom", "edge")))
    return jax.shard_map(local, mesh=mesh, in_specs=in_specs, out_specs=out_specs, check_vma=False)
```

```python
import jax
import jax.numpy as jnp
from jax import lax
from jax.experimental import pallas as pl
from jax.experimental.pallas import tpu as pltpu
from jax.sharding import PartitionSpec as P

ROUNDS = 2
WIDTH = 400
LANES = 512
MAIN = 384
ROWS = 96
PACKED = 304
SLOTS = 512
BLOCK = 384
ENT = 1536
NEG = 1000
learning_rate = 0.1

MESH = pl.DeviceIdType.MESH
f32 = jnp.float32
bf16 = jnp.bfloat16


def flip(z, k):
    if k == 0:
        return z
    if k == 1:
        return z + 1 - 2 * (z % 2)
    if k == 2:
        return (z + 2) % 4
    return 3 - z


def pack_rest(rest):
    out = rest[0:16, :]
    for g in range(1, 6):
        out = out + pltpu.roll(rest[16 * g : 16 * g + 16, :], 16 * g, 1)
    return out


def rest_piece(rest, g):
    lane = lax.broadcasted_iota(jnp.int32, (16, 128), 1)
    piece = rest if g == 0 else pltpu.roll(rest, 128 - 16 * g, 1)
    return jnp.where(lane < 16, piece, 0.0)


def kernel(
    emb_hbm, state_hbm, source_hbm, target_hbm, negative_hbm, count_hbm, emb_out, state_out,
    emb_ref, state_ref, source_ref, target_ref, negative_ref, count_ref, idx_ref, E, G, state_col, idx_far, own_pk, Lo, Lp, To, Tp, hot, HS, Us, Ws, MT, tmp,
    PBs, PBr, OBs, OBr, YBs, YBr, GO, ZBs, ZBr, Sv, Gv,
    ss, r_own, r_par, r_parq, r_pb, r_ob, r_yb, r_zb, r_idx, r_in,
):
    d, e = lax.axis_index("dom"), lax.axis_index("edge")
    zh, x, c = d // 8, (d // 2) % 4, d % 2
    y, z = e // 4, e % 4

    def dev(zh_, c_, y_, z_):
        return (zh_ * 8 + x * 2 + c_, y_ * 4 + z_)

    yp, ym, yo = (y + 1) % 4, (y + 3) % 4, (y + 2) % 4
    up, down, sib = dev(zh, c, yp, z), dev(zh, c, ym, z), dev(zh, 1 - c, y, z)
    mover = zh != c

    barrier = pltpu.get_barrier_semaphore()
    for to in (up, down, sib) + tuple(dev(zh, c, y, flip(z, k)) for k in (1, 2, 3)):
        pl.semaphore_signal(barrier, inc=1, device_id=to, device_id_type=MESH)

    @pl.when(mover)
    def _():
        for k in range(4):
            pl.semaphore_signal(
                barrier, inc=1, device_id=dev(c, zh, y, flip(z, k)), device_id_type=MESH
            )

    started = []
    count = [0]

    def send(src, dst, sem, to, when=None):
        slot = count[0]
        count[0] += 1

        def make():
            return pltpu.make_async_remote_copy(
                src_ref=src, dst_ref=dst, send_sem=ss.at[slot], recv_sem=sem,
                device_id=to, device_id_type=MESH,
            )

        if when is None:
            make().start()
        else:
            pl.when(when)(lambda: make().start())
        started.append((make, when))

    def drain():
        for make, when in started:
            if when is None:
                make().wait_send()
            else:
                pl.when(when)(lambda make=make: make().wait_send())
        started.clear()

    def arrived(dst, sem, when=None):
        def wait():
            pltpu.make_async_remote_copy(
                src_ref=dst, dst_ref=dst, send_sem=ss.at[0], recv_sem=sem,
                device_id=sib, device_id_type=MESH,
            ).wait_recv()

        if when is None:
            wait()
        else:
            pl.when(when)(wait)

    loads = []
    for i, (src, dst) in enumerate(
        (
            (emb_hbm, emb_ref), (state_hbm, state_ref), (source_hbm, source_ref),
            (target_hbm, target_ref), (negative_hbm, negative_ref), (count_hbm, count_ref),
        )
    ):
        loads.append(pltpu.make_async_copy(src, dst, r_in.at[i]))
        loads[-1].start()
    idx_ref[...] = jnp.full((ROUNDS, 8, SLOTS), -1, jnp.int32)
    for load in loads:
        load.wait()
    for r in range(ROUNDS):
        idx_ref[r, 0:1, :] = source_ref[r : r + 1, :]
        idx_ref[r, 1:2, :] = target_ref[r : r + 1, :]
        idx_ref[r, 2:3, :] = negative_ref[r : r + 1, :SLOTS]
        idx_ref[r, 3:4, : NEG - SLOTS] = negative_ref[r : r + 1, SLOTS:]
        idx_ref[r, 4:5, :] = jnp.broadcast_to(count_ref[:, r : r + 1], (1, SLOTS))

    E[:, MAIN:] = jnp.zeros((ROWS, LANES - MAIN), f32)
    E[:, :WIDTH] = emb_ref[...]
    diag = lax.broadcasted_iota(jnp.int32, (ROWS, ROWS), 0) == lax.broadcasted_iota(
        jnp.int32, (ROWS, ROWS), 1
    )
    state_col[...] = jnp.sum(
        jnp.where(diag, jnp.broadcast_to(state_ref[...], (ROWS, ROWS)), 0.0), axis=1, keepdims=True
    )

    def pack_own(r):
        for g in range(3):
            own_pk[r, ROWS * g : ROWS * (g + 1), :] = E[:, 128 * g : 128 * (g + 1)].astype(bf16)
        rest = E[:, MAIN:].astype(bf16).astype(f32)
        own_pk[r, 3 * ROWS :, :] = pack_rest(rest).astype(bf16)

    def row_of(r, i):
        return (idx_ref[0, i : i + 1, :] if r == 0 else idx_far[i : i + 1, :]).astype(f32)

    def source_hot(r):
        column = jnp.transpose(jnp.broadcast_to(row_of(r, 0), (128, SLOTS)))
        lane = lax.broadcasted_iota(jnp.int32, (SLOTS, 128), 1)
        for b, block in enumerate((y, yp, ym, yo)):
            for t in range(3):
                at = (lane + (block * BLOCK + 128 * t)).astype(f32)
                hot[b, :, 128 * t : 128 * (t + 1)] = jnp.where(column == at, 1.0, 0.0).astype(bf16)

    def scatter_hot(r):
        source = row_of(r, 0)
        row = lax.broadcasted_iota(jnp.int32, (128, SLOTS), 0)

        @pl.loop(0, ENT // 128)
        def _(i):
            at = (row + i * 128).astype(f32)
            HS[pl.ds(i * 128, 128), :] = jnp.where(source == at, 1.0, 0.0).astype(bf16)

    def multiplicity(r):
        first, second = row_of(r, 2), row_of(r, 3)
        target = row_of(r, 1)
        slot_at = lax.broadcasted_iota(jnp.int32, (1, SLOTS), 1).astype(f32)
        live = jnp.where(slot_at < row_of(r, 4), 0.5, 0.0)
        row = lax.broadcasted_iota(jnp.int32, (128, SLOTS), 0)

        @pl.loop(0, ENT // 128)
        def _(i):
            at = (row + i * 128).astype(f32)
            total = jnp.where(first == at, 1.0, 0.0) + jnp.where(second == at, 1.0, 0.0)
            share = jnp.sum(total, axis=1, keepdims=True) * (1.0 / NEG)
            same = jnp.where(target == at, 1.0, 0.0)
            Us[pl.ds(i * 128, 128), :] = live * (share + same)
            Ws[pl.ds(i * 128, 128), :] = live * (share - same)

    def assemble(L, T, r, slot):
        base = slot * ROWS
        for g in range(3):
            T[pl.ds(base, ROWS), 128 * g : 128 * (g + 1)] = L[r, slot, ROWS * g : ROWS * (g + 1), :]
        rest = L[r, slot, 3 * ROWS :, :].astype(f32)
        for g in range(6):
            T[pl.ds(base + 16 * g, 16), MAIN:] = rest_piece(rest, g).astype(bf16)

    def pack_chunk(ref, at):
        base = at * ROWS
        pieces = [ref[pl.ds(base, ROWS), 128 * g : 128 * (g + 1)] for g in range(3)]
        return pieces + [pack_rest(ref[pl.ds(base, ROWS), MAIN:])]

    spans = [(0, ROWS), (ROWS, 2 * ROWS), (2 * ROWS, 3 * ROWS), (3 * ROWS, PACKED)]

    for r in range(ROUNDS):
        far = mover if r == 1 else None
        zt, ct = (zh, c) if r == 0 else (c, zh)
        stay = None if r == 0 else jnp.logical_not(mover)

        pack_own(r)

        def keep(r=r):
            Lo[r, e] = own_pk[r]

        if r == 0:
            keep()
            pl.semaphore_wait(barrier, 6 + 4 * ((zh + c) % 2))
        else:
            pl.when(stay)(keep)
        def place(k, r=r):
            near = flip(z, k)
            return near if r == 0 else near + ((zh + c) % 2) * (3 - 2 * near)

        def turn(k, r=r):
            if k % 2 == 0:
                return flip(z, k)
            a, b = flip(z, k), flip(z, 4 - k)
            return a if r == 0 else a + ((zh + c) % 2) * (b - a)

        for k in range(4):
            if k > 0 or r == 1:
                send(
                    own_pk.at[r], Lo.at[r, e], r_own.at[r, e], dev(zt, ct, y, turn(k)),
                    mover if k == 0 else None,
                )

        def block_wait(block, k, to=None):
            slot = block * 4 + turn(k)
            arrived(Lo.at[r, slot], r_own.at[r, slot])
            if to is not None:
                send(Lo.at[r, slot], Lo.at[r, slot], r_own.at[r, slot], to)

        def line(k):
            slot = y * 4 + turn(k)
            if k > 0:
                arrived(Lo.at[r, slot], r_own.at[r, slot])
            elif r == 1:
                arrived(Lo.at[r, slot], r_own.at[r, slot], mover)
            send(Lo.at[r, slot], Lo.at[r, slot], r_own.at[r, slot], up)
            send(Lo.at[r, slot], Lo.at[r, slot], r_own.at[r, slot], down)

        def sibling_block(block, q):
            send(Lo.at[r, pl.ds(block * 4, 4)], Lp.at[r, pl.ds(block * 4, 4)], r_par.at[r, q], sib)

        def opposite(k):
            slot = yo * 4 + turn(k)
            arrived(Lo.at[r, slot], r_own.at[r, slot])
            send(Lo.at[r, slot], Lp.at[r, slot], r_parq.at[r, turn(k)], sib)

        def sources(b, block):
            for k in range(4):
                assemble(Lo, To, r, block * 4 + k)
            rows = To[pl.ds(pl.multiple_of(block * BLOCK, BLOCK), BLOCK), :]
            part = jnp.dot(hot[b], rows, preferred_element_type=f32)
            Sv[...] = part if b == 0 else Sv[...] + part

        def partner(q, block):
            arrived(Lp.at[r, pl.ds(block * 4, 4)], r_par.at[r, q])
            for k in range(4):
                assemble(Lp, Tp, r, block * 4 + k)

        line(0)
        if r == 0:
            send(idx_ref.at[1], idx_far, r_idx.at[0], dev(c, zh, y, z), mover)

            @pl.when(jnp.logical_not(mover))
            def _():
                idx_far[...] = idx_ref[1]

            source_hot(0)
            multiplicity(0)
        else:
            arrived(idx_far, r_idx.at[0], mover)
            source_hot(1)
        line(1)
        if r == 1:
            multiplicity(1)
        line(2)
        scatter_hot(r)
        line(3)
        sibling_block(y, 0)
        block_wait(ym, 0, up)
        block_wait(yp, 0)
        block_wait(yp, 1, down)
        block_wait(ym, 1)
        block_wait(ym, 2, up)
        block_wait(yp, 2)
        block_wait(yp, 3, down)
        block_wait(ym, 3)
        sibling_block(ym, 1)
        sibling_block(yp, 2)
        opposite(0)
        opposite(1)
        sources(0, y)
        sources(1, yp)
        partner(0, y)
        sources(2, ym)
        partner(1, ym)
        opposite(2)
        opposite(3)
        partner(2, yp)
        sources(3, yo)
        for k in range(4):
            slot = yo * 4 + turn(k)
            arrived(Lp.at[r, slot], r_parq.at[r, turn(k)])
            assemble(Lp, Tp, r, slot)

        half = (Sv[...] * 0.5).astype(bf16)
        def weights(i, held):
            rows = pl.ds(pl.multiple_of(i * BLOCK, BLOCK), BLOCK)
            t = jnp.tanh(
                lax.dot_general(
                    Tp[rows, :], half, (((1,), (1,)), ((), ())), preferred_element_type=f32
                )
            )
            slope, level = Us[rows, :], Ws[rows, :]
            m = slope * t + level
            weight = m.astype(bf16)
            MT[rows, :] = weight
            return held + jnp.sum((slope - level) * m, axis=0, keepdims=True)

        held = lax.fori_loop(0, ENT // BLOCK, weights, jnp.zeros((1, SLOTS), f32), unroll=True)
        rounded = held.astype(bf16).astype(f32)
        ratio = jnp.where(rounded == 0.0, 1.0, held / jnp.where(rounded == 0.0, 1.0, rounded))
        ratio = jnp.transpose(jnp.broadcast_to(ratio, (128, SLOTS)))
        ratio = jnp.concatenate([ratio] * (LANES // 128), axis=1)

        scaled = (Sv[...] * ratio).astype(bf16)

        def peer(b, block):
            rows = pl.ds(pl.multiple_of(block * BLOCK, BLOCK), BLOCK)
            tmp[...] = jnp.dot(MT[rows, :], scaled, preferred_element_type=f32)
            for k in range(4):
                for (lo, hi), piece in zip(spans, pack_chunk(tmp, k)):
                    PBs[r, b, k, lo:hi, :] = piece.astype(bf16)
            send(PBs.at[r, b], PBr.at[r, b], r_pb.at[r, b], sib)

        def own(b, block):
            rows = pl.ds(pl.multiple_of(block * BLOCK, BLOCK), BLOCK)
            tmp[...] = jnp.dot(HS[rows, :], grad, preferred_element_type=f32)
            arrived(PBr.at[r, b], r_pb.at[r, b])
            for k in (3, 2, 1, 0):
                for (lo, hi), piece in zip(spans, pack_chunk(tmp, place(k))):
                    total = piece + PBr[r, b, place(k), lo:hi, :].astype(f32)
                    if b == 0:
                        OBs[r, k, lo:hi, :] = total.astype(bf16)
                    elif b < 3 and k % 2 == b % 2:
                        YBs[r, b - 1, k, lo:hi, :] = total.astype(bf16)
                    else:
                        GO[b - 1, k, lo:hi, :] = total

        def send_opposite(k):
            send(OBs.at[r, k], OBr.at[r, k], r_ob.at[r, k], up if k % 2 == 0 else down)

        def send_block(q, k):
            send(YBs.at[r, q, k], YBr.at[r, q, k], r_yb.at[r, q, k], up if q == 0 else down)

        def add_opposite(k):
            q = k % 2
            arrived(OBr.at[r, k], r_ob.at[r, k])
            YBs[r, q, k] = (GO[q, k] + OBr[r, k].astype(f32)).astype(bf16)
            send_block(q, k)

        def to_line(k):
            arrived(YBr.at[r, 0, k], r_yb.at[r, 0, k])
            arrived(YBr.at[r, 1, k], r_yb.at[r, 1, k])
            GO[2, k] = GO[2, k] + YBr[r, 0, k].astype(f32) + YBr[r, 1, k].astype(f32)
            if k > 0 or r == 1:
                ZBs[r, k] = GO[2, k].astype(bf16)
                send(
                    ZBs.at[r, k], ZBr.at[r, k], r_zb.at[r, k], dev(zt, ct, y, place(k)),
                    None if k > 0 else mover,
                )

        peer(0, yo)
        grad = lax.dot_general(
            MT[...], Tp[...], (((0,), (0,)), ((), ())), preferred_element_type=f32
        )
        grad = (grad * ratio).astype(bf16)
        own(0, yo)
        send_opposite(3)
        send_opposite(2)
        send_opposite(1)
        send_opposite(0)
        peer(1, yp)
        peer(2, ym)
        own(1, yp)
        send_block(0, 3)
        own(2, ym)
        send_block(1, 2)
        peer(3, y)
        add_opposite(2)
        add_opposite(3)
        send_block(0, 1)
        send_block(1, 0)
        own(3, y)
        to_line(3)
        to_line(2)
        add_opposite(0)
        add_opposite(1)
        to_line(1)
        to_line(0)
        if r == ROUNDS - 1:
            drain()
        if r == 1:
            arrived(ZBr.at[r, 0], r_zb.at[r, 0], mover)

            @pl.when(mover)
            def _():
                GO[2, 0] = ZBr[1, 0].astype(f32)

        total = GO[2, 0]
        for k in (1, 2, 3):
            arrived(ZBr.at[r, k], r_zb.at[r, k])
            total = total + ZBr[r, k].astype(f32)

        for g in range(3):
            G[:, 128 * g : 128 * (g + 1)] = total[ROWS * g : ROWS * (g + 1), :]
        for g in range(6):
            G[16 * g : 16 * g + 16, MAIN:] = rest_piece(total[3 * ROWS :, :], g)
        grads = G[...]
        state = state_col[...] + jnp.sum(grads * grads, axis=1, keepdims=True) * (1.0 / WIDTH)
        state_col[...] = state
        E[...] = E[...] - grads * (learning_rate / jnp.sqrt(state))

    emb_out[...] = E[:, :WIDTH]
    state_out[...] = jnp.sum(
        jnp.where(diag, jnp.broadcast_to(state_col[...], (ROWS, ROWS)), 0.0), axis=0, keepdims=True
    )
    drain()


def local(embeddings, adagrad_state, source_rows, target_rows, negative_rows, edge_counts):
    vmem = pl.BlockSpec(memory_space=pltpu.VMEM)
    DMA = pltpu.SemaphoreType.DMA
    table, state = pl.pallas_call(
        kernel,
        name="bucket_rounds",
        out_shape=(
            pltpu.VMEM((ROWS, WIDTH), f32),
            pltpu.VMEM((1, ROWS), f32),
        ),
        in_specs=[pl.BlockSpec(memory_space=pl.ANY)] * 6,
        out_specs=(vmem, vmem),
        scratch_shapes=[
            pltpu.VMEM((ROWS, WIDTH), f32),
            pltpu.VMEM((1, ROWS), f32),
            pltpu.VMEM((ROUNDS, SLOTS), jnp.int32),
            pltpu.VMEM((ROUNDS, SLOTS), jnp.int32),
            pltpu.VMEM((ROUNDS, NEG), jnp.int32),
            pltpu.VMEM((1, ROUNDS), jnp.int32),
            pltpu.VMEM((ROUNDS, 8, SLOTS), jnp.int32),
            pltpu.VMEM((ROWS, LANES), f32),
            pltpu.VMEM((ROWS, LANES), f32),
            pltpu.VMEM((ROWS, 1), f32),
            pltpu.VMEM((8, SLOTS), jnp.int32),
            pltpu.VMEM((ROUNDS, PACKED, 128), bf16),
            pltpu.VMEM((ROUNDS, 16, PACKED, 128), bf16),
            pltpu.VMEM((ROUNDS, 16, PACKED, 128), bf16),
            pltpu.VMEM((ENT, LANES), bf16),
            pltpu.VMEM((ENT, LANES), bf16),
            pltpu.VMEM((4, SLOTS, BLOCK), bf16),
            pltpu.VMEM((ENT, SLOTS), bf16),
            pltpu.VMEM((ENT, SLOTS), f32),
            pltpu.VMEM((ENT, SLOTS), f32),
            pltpu.VMEM((ENT, SLOTS), bf16),
            pltpu.VMEM((BLOCK, LANES), f32),
            pltpu.VMEM((ROUNDS, 4, 4, PACKED, 128), bf16),
            pltpu.VMEM((ROUNDS, 4, 4, PACKED, 128), bf16),
            pltpu.VMEM((ROUNDS, 4, PACKED, 128), bf16),
            pltpu.VMEM((ROUNDS, 4, PACKED, 128), bf16),
            pltpu.VMEM((ROUNDS, 2, 4, PACKED, 128), bf16),
            pltpu.VMEM((ROUNDS, 2, 4, PACKED, 128), bf16),
            pltpu.VMEM((3, 4, PACKED, 128), f32),
            pltpu.VMEM((ROUNDS, 4, PACKED, 128), bf16),
            pltpu.VMEM((ROUNDS, 4, PACKED, 128), bf16),
            pltpu.VMEM((SLOTS, LANES), f32),
            pltpu.VMEM((SLOTS, LANES), f32),
            DMA((104,)),
            DMA((ROUNDS, 16)),
            DMA((ROUNDS, 3)),
            DMA((ROUNDS, 4)),
            DMA((ROUNDS, 4)),
            DMA((ROUNDS, 4)),
            DMA((ROUNDS, 2, 4)),
            DMA((ROUNDS, 4)),
            DMA((1,)),
            DMA((6,)),
        ],
        compiler_params=pltpu.CompilerParams(
            collective_id=0, has_side_effects=True, vmem_limit_bytes=56 * 1024 * 1024
        ),
        cost_estimate=pl.CostEstimate(
            flops=2 * ROUNDS * 5 * ENT * SLOTS * WIDTH,
            bytes_accessed=4 * ROWS * WIDTH * 2,
            transcendentals=ROUNDS * ENT * SLOTS,
        ),
    )(
        embeddings,
        adagrad_state.reshape(1, ROWS),
        source_rows,
        target_rows,
        negative_rows,
        edge_counts.reshape(1, ROUNDS),
    )
    return table, state.reshape(ROWS)


def solution(mesh):
    in_specs = (
        P(("dom", "edge"), None),
        P(("dom", "edge")),
        P(None, ("dom", "edge")),
        P(None, ("dom", "edge")),
        P(None, ("dom", "edge")),
        P(None, ("dom", "edge")),
    )
    out_specs = (P(("dom", "edge"), None), P(("dom", "edge")))
    return jax.shard_map(local, mesh=mesh, in_specs=in_specs, out_specs=out_specs, check_vma=False)
```

```python
import jax
import jax.numpy as jnp
from jax import lax
from jax.experimental import pallas as pl
from jax.experimental.pallas import tpu as pltpu
from jax.sharding import PartitionSpec as P

ROUNDS = 2
WIDTH = 400
LANES = 512
MAIN = 384
ROWS = 96
PACKED = 304
SLOTS = 512
BLOCK = 384
ENT = 1536
NEG = 1000
learning_rate = 0.1

MESH = pl.DeviceIdType.MESH
f32 = jnp.float32
bf16 = jnp.bfloat16


def flip(z, k):
    if k == 0:
        return z
    if k == 1:
        return z + 1 - 2 * (z % 2)
    if k == 2:
        return (z + 2) % 4
    return 3 - z


def pack_rest(rest):
    out = rest[0:16, :]
    for g in range(1, 6):
        out = out + pltpu.roll(rest[16 * g : 16 * g + 16, :], 16 * g, 1)
    return out


def rest_piece(rest, g):
    lane = lax.broadcasted_iota(jnp.int32, (16, 128), 1)
    piece = rest if g == 0 else pltpu.roll(rest, 128 - 16 * g, 1)
    return jnp.where(lane < 16, piece, 0.0)


def kernel(
    emb_hbm, state_hbm, source_hbm, target_hbm, negative_hbm, count_hbm, emb_out, state_out,
    emb_ref, state_ref, source_ref, target_ref, negative_ref, count_ref, idx_ref, E, G, state_col, idx_far, own_pk, Lo, Lp, To, Tp, hot, HS, Us, Ws, MT, tmp,
    PBs, PBr, OBs, OBr, YBs, YBr, GO, ZBs, ZBr, Sv, Gv,
    ss, r_own, r_par, r_parq, r_pb, r_ob, r_yb, r_zb, r_idx, r_in,
):
    d, e = lax.axis_index("dom"), lax.axis_index("edge")
    zh, x, c = d // 8, (d // 2) % 4, d % 2
    y, z = e // 4, e % 4

    def dev(zh_, c_, y_, z_):
        return (zh_ * 8 + x * 2 + c_, y_ * 4 + z_)

    yp, ym, yo = (y + 1) % 4, (y + 3) % 4, (y + 2) % 4
    up, down, sib = dev(zh, c, yp, z), dev(zh, c, ym, z), dev(zh, 1 - c, y, z)
    mover = zh != c

    barrier = pltpu.get_barrier_semaphore()
    for to in (up, down, sib) + tuple(dev(zh, c, y, flip(z, k)) for k in (1, 2, 3)):
        pl.semaphore_signal(barrier, inc=1, device_id=to, device_id_type=MESH)

    @pl.when(mover)
    def _():
        for k in range(4):
            pl.semaphore_signal(
                barrier, inc=1, device_id=dev(c, zh, y, flip(z, k)), device_id_type=MESH
            )

    started = []
    count = [0]

    def send(src, dst, sem, to, when=None):
        slot = count[0]
        count[0] += 1

        def make():
            return pltpu.make_async_remote_copy(
                src_ref=src, dst_ref=dst, send_sem=ss.at[slot], recv_sem=sem,
                device_id=to, device_id_type=MESH,
            )

        if when is None:
            make().start()
        else:
            pl.when(when)(lambda: make().start())
        started.append((make, when))

    def drain():
        for make, when in started:
            if when is None:
                make().wait_send()
            else:
                pl.when(when)(lambda make=make: make().wait_send())
        started.clear()

    def arrived(dst, sem, when=None):
        def wait():
            pltpu.make_async_remote_copy(
                src_ref=dst, dst_ref=dst, send_sem=ss.at[0], recv_sem=sem,
                device_id=sib, device_id_type=MESH,
            ).wait_recv()

        if when is None:
            wait()
        else:
            pl.when(when)(wait)

    loads = []
    for i, (src, dst) in enumerate(
        (
            (emb_hbm, emb_ref), (state_hbm, state_ref), (source_hbm, source_ref),
            (target_hbm, target_ref), (negative_hbm, negative_ref), (count_hbm, count_ref),
        )
    ):
        loads.append(pltpu.make_async_copy(src, dst, r_in.at[i]))
        loads[-1].start()
    loads[0].wait()

    E[:, MAIN:] = jnp.zeros((ROWS, LANES - MAIN), f32)
    E[:, :WIDTH] = emb_ref[...]
    diag = lax.broadcasted_iota(jnp.int32, (ROWS, ROWS), 0) == lax.broadcasted_iota(
        jnp.int32, (ROWS, ROWS), 1
    )
    def pack_own(r):
        for g in range(3):
            own_pk[r, ROWS * g : ROWS * (g + 1), :] = E[:, 128 * g : 128 * (g + 1)].astype(bf16)
        rest = E[:, MAIN:].astype(bf16).astype(f32)
        own_pk[r, 3 * ROWS :, :] = pack_rest(rest).astype(bf16)

    def row_of(r, i):
        return (idx_ref[0, i : i + 1, :] if r == 0 else idx_far[i : i + 1, :]).astype(f32)

    def source_hot(r):
        column = jnp.transpose(jnp.broadcast_to(row_of(r, 0), (128, SLOTS)))
        lane = lax.broadcasted_iota(jnp.int32, (SLOTS, 128), 1)
        for b, block in enumerate((y, yp, ym, yo)):
            for t in range(3):
                at = (lane + (block * BLOCK + 128 * t)).astype(f32)
                hot[b, :, 128 * t : 128 * (t + 1)] = jnp.where(column == at, 1.0, 0.0).astype(bf16)

    def scatter_hot(r):
        source = row_of(r, 0)
        row = lax.broadcasted_iota(jnp.int32, (128, SLOTS), 0)

        @pl.loop(0, ENT // 128)
        def _(i):
            at = (row + i * 128).astype(f32)
            HS[pl.ds(i * 128, 128), :] = jnp.where(source == at, 1.0, 0.0).astype(bf16)

    def multiplicity(r):
        first, second = row_of(r, 2), row_of(r, 3)
        target = row_of(r, 1)
        slot_at = lax.broadcasted_iota(jnp.int32, (1, SLOTS), 1).astype(f32)
        live = jnp.where(slot_at < row_of(r, 4), 0.5, 0.0)
        row = lax.broadcasted_iota(jnp.int32, (128, SLOTS), 0)

        @pl.loop(0, ENT // 128)
        def _(i):
            at = (row + i * 128).astype(f32)
            total = jnp.where(first == at, 1.0, 0.0) + jnp.where(second == at, 1.0, 0.0)
            share = jnp.sum(total, axis=1, keepdims=True) * (1.0 / NEG)
            same = jnp.where(target == at, 1.0, 0.0)
            Us[pl.ds(i * 128, 128), :] = live * (share + same)
            Ws[pl.ds(i * 128, 128), :] = live * (share - same)

    def assemble(L, T, r, slot):
        base = slot * ROWS
        for g in range(3):
            T[pl.ds(base, ROWS), 128 * g : 128 * (g + 1)] = L[r, slot, ROWS * g : ROWS * (g + 1), :]
        rest = L[r, slot, 3 * ROWS :, :].astype(f32)
        for g in range(6):
            T[pl.ds(base + 16 * g, 16), MAIN:] = rest_piece(rest, g).astype(bf16)

    def pack_chunk(ref, at):
        base = at * ROWS
        pieces = [ref[pl.ds(base, ROWS), 128 * g : 128 * (g + 1)] for g in range(3)]
        return pieces + [pack_rest(ref[pl.ds(base, ROWS), MAIN:])]

    spans = [(0, ROWS), (ROWS, 2 * ROWS), (2 * ROWS, 3 * ROWS), (3 * ROWS, PACKED)]

    for r in range(ROUNDS):
        far = mover if r == 1 else None
        zt, ct = (zh, c) if r == 0 else (c, zh)
        stay = None if r == 0 else jnp.logical_not(mover)

        pack_own(r)

        def keep(r=r):
            Lo[r, e] = own_pk[r]

        if r == 0:
            keep()
            pl.semaphore_wait(barrier, 6 + 4 * ((zh + c) % 2))
        else:
            pl.when(stay)(keep)
        def place(k, r=r):
            near = flip(z, k)
            return near if r == 0 else near + ((zh + c) % 2) * (3 - 2 * near)

        def turn(k, r=r):
            if k % 2 == 0:
                return flip(z, k)
            a, b = flip(z, k), flip(z, 4 - k)
            return a if r == 0 else a + ((zh + c) % 2) * (b - a)

        def line(k):
            slot = y * 4 + turn(k)
            if k > 0:
                arrived(Lo.at[r, slot], r_own.at[r, slot])
            elif r == 1:
                arrived(Lo.at[r, slot], r_own.at[r, slot], mover)
            send(Lo.at[r, slot], Lo.at[r, slot], r_own.at[r, slot], up)
            send(Lo.at[r, slot], Lo.at[r, slot], r_own.at[r, slot], down)

        if r == 0:
            line(0)
        for k in range(4):
            if k > 0 or r == 1:
                send(
                    own_pk.at[r], Lo.at[r, e], r_own.at[r, e], dev(zt, ct, y, turn(k)),
                    mover if k == 0 else None,
                )

        def block_wait(block, k, to=None):
            slot = block * 4 + turn(k)
            arrived(Lo.at[r, slot], r_own.at[r, slot])
            if to is not None:
                send(Lo.at[r, slot], Lo.at[r, slot], r_own.at[r, slot], to)

        def sibling_block(block, q):
            send(Lo.at[r, pl.ds(block * 4, 4)], Lp.at[r, pl.ds(block * 4, 4)], r_par.at[r, q], sib)

        def opposite(k):
            slot = yo * 4 + turn(k)
            arrived(Lo.at[r, slot], r_own.at[r, slot])
            send(Lo.at[r, slot], Lp.at[r, slot], r_parq.at[r, turn(k)], sib)

        def sources(b, block):
            for k in range(4):
                assemble(Lo, To, r, block * 4 + k)
            rows = To[pl.ds(pl.multiple_of(block * BLOCK, BLOCK), BLOCK), :]
            part = jnp.dot(hot[b], rows, preferred_element_type=f32)
            Sv[...] = part if b == 0 else Sv[...] + part

        def partner(q, block):
            arrived(Lp.at[r, pl.ds(block * 4, 4)], r_par.at[r, q])
            for k in range(4):
                assemble(Lp, Tp, r, block * 4 + k)

        if r == 1:
            line(0)
        if r == 0:
            idx_ref[...] = jnp.full((ROUNDS, 8, SLOTS), -1, jnp.int32)
            for load in loads[1:]:
                load.wait()
            for q in range(ROUNDS):
                idx_ref[q, 0:1, :] = source_ref[q : q + 1, :]
                idx_ref[q, 1:2, :] = target_ref[q : q + 1, :]
                idx_ref[q, 2:3, :] = negative_ref[q : q + 1, :SLOTS]
                idx_ref[q, 3:4, : NEG - SLOTS] = negative_ref[q : q + 1, SLOTS:]
                idx_ref[q, 4:5, :] = jnp.broadcast_to(count_ref[:, q : q + 1], (1, SLOTS))
            state_col[...] = jnp.sum(
                jnp.where(diag, jnp.broadcast_to(state_ref[...], (ROWS, ROWS)), 0.0), axis=1, keepdims=True
            )
            send(idx_ref.at[1], idx_far, r_idx.at[0], dev(c, zh, y, z), mover)

            @pl.when(jnp.logical_not(mover))
            def _():
                idx_far[...] = idx_ref[1]

            source_hot(0)
            multiplicity(0)
        else:
            arrived(idx_far, r_idx.at[0], mover)
            source_hot(1)
        line(1)
        if r == 1:
            multiplicity(1)
        line(2)
        scatter_hot(r)
        line(3)
        sibling_block(y, 0)
        block_wait(ym, 0, up)
        block_wait(yp, 0)
        block_wait(yp, 1, down)
        block_wait(ym, 1)
        block_wait(ym, 2, up)
        block_wait(yp, 2)
        block_wait(yp, 3, down)
        block_wait(ym, 3)
        sibling_block(ym, 1)
        sibling_block(yp, 2)
        opposite(0)
        opposite(1)
        sources(0, y)
        sources(1, yp)
        partner(0, y)
        sources(2, ym)
        partner(1, ym)
        opposite(2)
        opposite(3)
        partner(2, yp)
        sources(3, yo)
        for k in range(4):
            slot = yo * 4 + turn(k)
            arrived(Lp.at[r, slot], r_parq.at[r, turn(k)])
            assemble(Lp, Tp, r, slot)

        half = (Sv[...] * 0.5).astype(bf16)
        def weights(i, held):
            rows = pl.ds(pl.multiple_of(i * BLOCK, BLOCK), BLOCK)
            t = jnp.tanh(
                lax.dot_general(
                    Tp[rows, :], half, (((1,), (1,)), ((), ())), preferred_element_type=f32
                )
            )
            slope, level = Us[rows, :], Ws[rows, :]
            m = slope * t + level
            weight = m.astype(bf16)
            MT[rows, :] = weight
            return held + jnp.sum((slope - level) * m, axis=0, keepdims=True)

        held = lax.fori_loop(0, ENT // BLOCK, weights, jnp.zeros((1, SLOTS), f32), unroll=True)
        rounded = held.astype(bf16).astype(f32)
        ratio = jnp.where(rounded == 0.0, 1.0, held / jnp.where(rounded == 0.0, 1.0, rounded))
        ratio = jnp.transpose(jnp.broadcast_to(ratio, (128, SLOTS)))
        ratio = jnp.concatenate([ratio] * (LANES // 128), axis=1)

        scaled = (Sv[...] * ratio).astype(bf16)

        def peer(b, block):
            rows = pl.ds(pl.multiple_of(block * BLOCK, BLOCK), BLOCK)
            tmp[...] = jnp.dot(MT[rows, :], scaled, preferred_element_type=f32)
            for k in range(4):
                for (lo, hi), piece in zip(spans, pack_chunk(tmp, k)):
                    PBs[r, b, k, lo:hi, :] = piece.astype(bf16)
            send(PBs.at[r, b], PBr.at[r, b], r_pb.at[r, b], sib)

        def own(b, block):
            rows = pl.ds(pl.multiple_of(block * BLOCK, BLOCK), BLOCK)
            tmp[...] = jnp.dot(HS[rows, :], grad, preferred_element_type=f32)
            arrived(PBr.at[r, b], r_pb.at[r, b])
            for k in (3, 2, 1, 0):
                for (lo, hi), piece in zip(spans, pack_chunk(tmp, place(k))):
                    total = piece + PBr[r, b, place(k), lo:hi, :].astype(f32)
                    if b == 0:
                        OBs[r, k, lo:hi, :] = total.astype(bf16)
                    elif b < 3 and k % 2 == b % 2:
                        YBs[r, b - 1, k, lo:hi, :] = total.astype(bf16)
                    else:
                        GO[b - 1, k, lo:hi, :] = total

        def send_opposite(k):
            send(OBs.at[r, k], OBr.at[r, k], r_ob.at[r, k], up if k % 2 == 0 else down)

        def send_block(q, k):
            send(YBs.at[r, q, k], YBr.at[r, q, k], r_yb.at[r, q, k], up if q == 0 else down)

        def add_opposite(k):
            q = k % 2
            arrived(OBr.at[r, k], r_ob.at[r, k])
            YBs[r, q, k] = (GO[q, k] + OBr[r, k].astype(f32)).astype(bf16)
            send_block(q, k)

        def to_line(k):
            arrived(YBr.at[r, 0, k], r_yb.at[r, 0, k])
            arrived(YBr.at[r, 1, k], r_yb.at[r, 1, k])
            GO[2, k] = GO[2, k] + YBr[r, 0, k].astype(f32) + YBr[r, 1, k].astype(f32)
            if k > 0 or r == 1:
                ZBs[r, k] = GO[2, k].astype(bf16)
                send(
                    ZBs.at[r, k], ZBr.at[r, k], r_zb.at[r, k], dev(zt, ct, y, place(k)),
                    None if k > 0 else mover,
                )

        peer(0, yo)
        grad = lax.dot_general(
            MT[...], Tp[...], (((0,), (0,)), ((), ())), preferred_element_type=f32
        )
        grad = (grad * ratio).astype(bf16)
        own(0, yo)
        send_opposite(3)
        send_opposite(2)
        send_opposite(1)
        send_opposite(0)
        peer(1, yp)
        peer(2, ym)
        own(1, yp)
        send_block(0, 3)
        own(2, ym)
        send_block(1, 2)
        peer(3, y)
        add_opposite(2)
        add_opposite(3)
        send_block(0, 1)
        send_block(1, 0)
        own(3, y)
        to_line(3)
        to_line(2)
        add_opposite(0)
        add_opposite(1)
        to_line(1)
        to_line(0)
        if r == ROUNDS - 1:
            drain()
        if r == 1:
            arrived(ZBr.at[r, 0], r_zb.at[r, 0], mover)

            @pl.when(mover)
            def _():
                GO[2, 0] = ZBr[1, 0].astype(f32)

        total = GO[2, 0]
        for k in (1, 2, 3):
            arrived(ZBr.at[r, k], r_zb.at[r, k])
            total = total + ZBr[r, k].astype(f32)

        for g in range(3):
            G[:, 128 * g : 128 * (g + 1)] = total[ROWS * g : ROWS * (g + 1), :]
        for g in range(6):
            G[16 * g : 16 * g + 16, MAIN:] = rest_piece(total[3 * ROWS :, :], g)
        grads = G[...]
        state = state_col[...] + jnp.sum(grads * grads, axis=1, keepdims=True) * (1.0 / WIDTH)
        state_col[...] = state
        E[...] = E[...] - grads * (learning_rate / jnp.sqrt(state))

    emb_out[...] = E[:, :WIDTH]
    state_out[...] = jnp.sum(
        jnp.where(diag, jnp.broadcast_to(state_col[...], (ROWS, ROWS)), 0.0), axis=0, keepdims=True
    )
    drain()


def local(embeddings, adagrad_state, source_rows, target_rows, negative_rows, edge_counts):
    vmem = pl.BlockSpec(memory_space=pltpu.VMEM)
    DMA = pltpu.SemaphoreType.DMA
    table, state = pl.pallas_call(
        kernel,
        name="bucket_rounds",
        out_shape=(
            pltpu.VMEM((ROWS, WIDTH), f32),
            pltpu.VMEM((1, ROWS), f32),
        ),
        in_specs=[pl.BlockSpec(memory_space=pl.ANY)] * 6,
        out_specs=(vmem, vmem),
        scratch_shapes=[
            pltpu.VMEM((ROWS, WIDTH), f32),
            pltpu.VMEM((1, ROWS), f32),
            pltpu.VMEM((ROUNDS, SLOTS), jnp.int32),
            pltpu.VMEM((ROUNDS, SLOTS), jnp.int32),
            pltpu.VMEM((ROUNDS, NEG), jnp.int32),
            pltpu.VMEM((1, ROUNDS), jnp.int32),
            pltpu.VMEM((ROUNDS, 8, SLOTS), jnp.int32),
            pltpu.VMEM((ROWS, LANES), f32),
            pltpu.VMEM((ROWS, LANES), f32),
            pltpu.VMEM((ROWS, 1), f32),
            pltpu.VMEM((8, SLOTS), jnp.int32),
            pltpu.VMEM((ROUNDS, PACKED, 128), bf16),
            pltpu.VMEM((ROUNDS, 16, PACKED, 128), bf16),
            pltpu.VMEM((ROUNDS, 16, PACKED, 128), bf16),
            pltpu.VMEM((ENT, LANES), bf16),
            pltpu.VMEM((ENT, LANES), bf16),
            pltpu.VMEM((4, SLOTS, BLOCK), bf16),
            pltpu.VMEM((ENT, SLOTS), bf16),
            pltpu.VMEM((ENT, SLOTS), f32),
            pltpu.VMEM((ENT, SLOTS), f32),
            pltpu.VMEM((ENT, SLOTS), bf16),
            pltpu.VMEM((BLOCK, LANES), f32),
            pltpu.VMEM((ROUNDS, 4, 4, PACKED, 128), bf16),
            pltpu.VMEM((ROUNDS, 4, 4, PACKED, 128), bf16),
            pltpu.VMEM((ROUNDS, 4, PACKED, 128), bf16),
            pltpu.VMEM((ROUNDS, 4, PACKED, 128), bf16),
            pltpu.VMEM((ROUNDS, 2, 4, PACKED, 128), bf16),
            pltpu.VMEM((ROUNDS, 2, 4, PACKED, 128), bf16),
            pltpu.VMEM((3, 4, PACKED, 128), f32),
            pltpu.VMEM((ROUNDS, 4, PACKED, 128), bf16),
            pltpu.VMEM((ROUNDS, 4, PACKED, 128), bf16),
            pltpu.VMEM((SLOTS, LANES), f32),
            pltpu.VMEM((SLOTS, LANES), f32),
            DMA((104,)),
            DMA((ROUNDS, 16)),
            DMA((ROUNDS, 3)),
            DMA((ROUNDS, 4)),
            DMA((ROUNDS, 4)),
            DMA((ROUNDS, 4)),
            DMA((ROUNDS, 2, 4)),
            DMA((ROUNDS, 4)),
            DMA((1,)),
            DMA((6,)),
        ],
        compiler_params=pltpu.CompilerParams(
            collective_id=0, has_side_effects=True, vmem_limit_bytes=56 * 1024 * 1024
        ),
        cost_estimate=pl.CostEstimate(
            flops=2 * ROUNDS * 5 * ENT * SLOTS * WIDTH,
            bytes_accessed=4 * ROWS * WIDTH * 2,
            transcendentals=ROUNDS * ENT * SLOTS,
        ),
    )(
        embeddings,
        adagrad_state.reshape(1, ROWS),
        source_rows,
        target_rows,
        negative_rows,
        edge_counts.reshape(1, ROUNDS),
    )
    return table, state.reshape(ROWS)


def solution(mesh):
    in_specs = (
        P(("dom", "edge"), None),
        P(("dom", "edge")),
        P(None, ("dom", "edge")),
        P(None, ("dom", "edge")),
        P(None, ("dom", "edge")),
        P(None, ("dom", "edge")),
    )
    out_specs = (P(("dom", "edge"), None), P(("dom", "edge")))
    return jax.shard_map(local, mesh=mesh, in_specs=in_specs, out_specs=out_specs, check_vma=False)
```
